512 devices in a mesh: dom: 32 (over x, z), slab: 8 (over y), chan: 2 (over core).
Axes of the slice: x: 4, y: 8, z: 8, core: 2. Of those that a mesh axis runs over, the one named last changes fastest.
Arguments:
- point_features: bfloat16 [64, 2097152], P('chan', ('dom', 'slab')), may hold values from -0.8984375 to 0.8984375
- neighbour_cells: int32 [8, 2097152], P(None, ('dom', 'slab')), may hold values from 0 to 127
- neighbour_weights: float32 [8, 2097152], P(None, ('dom', 'slab')), may hold values from 0.1 to 1
- live_points: int32 [256], P(('dom', 'slab')), may hold values from 2048 to 8192, as said below
- tile_target: int32 [16384], P(('dom', 'slab')), may hold values from 0 to 127, as said below
- conv_kernel: bfloat16 [27, 64, 64], replicated, may hold values from -0.15625 to 0.15625
- cotangent: bfloat16 [64, 16, 64, 128], P('chan', 'slab', 'dom'), may hold values from -6 to 6
Outputs:
- latent: bfloat16 [64, 16, 64, 128], P('chan', 'slab', 'dom')
- feature_grad: bfloat16 [64, 2097152], P('chan', ('dom', 'slab'))
- kernel_grad: float32 [27, 64, 64], replicated
The draws below stay inside these ranges and needn't reach their ends.
Inputs may be any that keep to these rules, and one draw needn't show every extreme that they name: `live_points`: some partition has all its 8192 points live. Among the 64 tiles of one partition at most 4 have tile_target // 4 equal to any one dom index; in every slab some dom index gets exactly 4 tiles from every partition of that slab.
All inputs are finite; a program needn't handle non-finite values.
Results may differ from the reference program's by a relative error of at most 0.014.
Values may be sent and summed in bfloat16 or wider, within the bound.
No kernel may reach another device: no remote copies, remote signals or barrier semaphores. Data moves between devices by JAX's collectives and lax.ppermute only.
A program may use at most 64 MiB of HBM per device.

```python
import math
import jax
import jax.numpy as jnp
from jax import lax

C = 64
NZ = 128
TILE = 128
K = 8
XD = 2
YD = 2
PT = 64
NX = 16
NY = 64
PARTS_SIZE = 256
POINTS = 2097152
CAP = 4
N_SLAB = 8


def draw_live_points(key, part):
    key = jax.random.fold_in(key, 12)
    counts = jax.random.randint(jax.random.fold_in(key, 1), (PARTS_SIZE,), PT * TILE // 4, PT * TILE + 1)
    fullest = jax.random.randint(jax.random.fold_in(key, 2), (), 0, PARTS_SIZE)
    return counts.at[fullest].set(PT * TILE).astype(jnp.int32)


def draw_tile_target(key, part):
    key = jax.random.fold_in(key, 11)
    dom_count = NY // YD
    slab_count = NX // XD
    heavy = jax.random.randint(jax.random.fold_in(key, 1), (slab_count,), 0, dom_count)

    def one_partition(index):
        inner = jax.random.fold_in(key, index + 2)
        first = heavy[index % slab_count]
        places = jax.random.permutation(jax.random.fold_in(inner, 1), (dom_count - 1) * CAP)[:PT - CAP]
        others = (first + 1 + places // CAP) % dom_count
        owners = jnp.concatenate([jnp.full((CAP,), first, jnp.int32), others.astype(jnp.int32)])
        order = jax.random.permutation(jax.random.fold_in(inner, 2), PT)
        owners = owners[order]
        within = jax.random.randint(jax.random.fold_in(inner, 3), (PT,), 0, XD * YD)
        return owners * (XD * YD) + within
    return jax.vmap(one_partition)(jnp.arange(PARTS_SIZE, dtype=jnp.int32)).reshape(-1).astype(jnp.int32)


def touch_ends(result, own_key, smallest, top_value):
    extent = result.shape
    index_at = [jax.random.randint(jax.random.fold_in(own_key, axis), (), 0, extent[axis]) for axis in range(len(extent))]
    result = result.at[tuple(index_at)].set(smallest)
    longest = extent.index(max(extent))
    index_at[longest] = (index_at[longest] + 1) % extent[longest]
    return result.at[tuple(index_at)].set(top_value)


def steps_of(own_key, extent, split, low, top_value):
    def one(axis_at, blocks):
        steps = jax.random.uniform(jax.random.fold_in(jax.random.fold_in(own_key, 6), axis_at), (blocks,), jnp.float32, low / len(split), top_value / len(split))
        return jnp.repeat(jnp.exp(steps), extent[axis_at] // blocks).reshape((-1,) + (1,) * (len(extent) - axis_at - 1))

    level = one(*split[0])
    for cut in split[1:]:
        level = level * one(*cut)
    return level


def normal_values(stream_key, dims, scale, bound, shards=(), kind=jnp.bfloat16):
    entries = scale * jax.random.normal(stream_key, dims, jnp.float32)
    if shards:
        entries = entries * steps_of(stream_key, dims, shards, -0.22, 0.18)
    return jnp.clip(entries, -bound, bound).astype(kind)


def setup_inputs(seed: int = 0) -> dict:
    key_list = jax.random.split(jax.random.key(seed), 8)
    point_features = normal_values(key_list[0], (C, POINTS), 0.15, 0.8984375, ((0, 2), (1, 256)))
    neighbour_cells = touch_ends(jax.random.randint(key_list[1], (K, POINTS), 0, NZ), jax.random.fold_in(key_list[1], 1), 0, NZ - 1).astype(jnp.int32)
    neighbour_weights = jnp.clip(jnp.exp(math.log(1.0) - 2.3025851 * jax.random.uniform(key_list[2], (K, POINTS), jnp.float32) ** steps_of(key_list[2], (K, POINTS), ((1, 256),), -0.2, 0.2)), 0.1, 1.0)
    live_points = draw_live_points(jax.random.fold_in(key_list[7], 71), 0)
    tile_target = draw_tile_target(jax.random.fold_in(key_list[7], 71), 0)
    conv_kernel = normal_values(key_list[5], (27, C, C), (27 * C) ** -0.5, 0.15625)
    cotangent = normal_values(key_list[6], (C, NX, NY, NZ), 1.0, 6.0, ((0, 2), (1, 8), (2, 32)))
    return dict(point_features=point_features, neighbour_cells=neighbour_cells, neighbour_weights=neighbour_weights, live_points=live_points, tile_target=tile_target, conv_kernel=conv_kernel, cotangent=cotangent)


def point_entries(cells, weights, alive):
    values = []
    for first_k in range(cells.shape[0]):
        total = jnp.zeros(cells.shape[1:], jnp.float32)
        unique = alive
        for other in range(cells.shape[0]):
            same = cells[other] == cells[first_k]
            total = total + jnp.where(same, weights[other], jnp.float32(0.0)).astype(jnp.float32)
            if other < first_k:
                unique = unique & jnp.logical_not(same)
        rounded = lax.optimization_barrier(total.astype(jnp.bfloat16)).astype(jnp.float32)
        values.append(jnp.where(unique, rounded, jnp.float32(0.0)))
    return values


def partition_data(index, neighbour_cells, neighbour_weights, live_points, tile_target):
    per = PT * TILE
    start = (index * per).astype(jnp.int32)
    cells = lax.dynamic_slice_in_dim(neighbour_cells, start, per, 1)
    weights = lax.dynamic_slice_in_dim(neighbour_weights, start, per, 1).astype(jnp.float32)
    alive = jnp.arange(per, dtype=jnp.int32) < live_points[index]
    columns = jnp.repeat(lax.dynamic_slice_in_dim(tile_target, (index * PT).astype(jnp.int32), PT, 0), TILE)
    slab_index = index % N_SLAB
    grid_x = slab_index * XD + columns % XD
    grid_y = columns // XD
    base = ((grid_x * NY + grid_y) * NZ).astype(jnp.int32)
    values = point_entries(cells, weights, alive)
    return start, cells, base, values


def reference(point_features, neighbour_cells, neighbour_weights, live_points, tile_target, conv_kernel, cotangent):
    per = PT * TILE
    parts = live_points.shape[0]
    cells_all = NX * NY * NZ

    def pool_one(index, grid):
        index = jnp.asarray(index).astype(jnp.int32)
        start, cells, base, values = partition_data(index, neighbour_cells, neighbour_weights, live_points, tile_target)
        feats = lax.dynamic_slice_in_dim(point_features, start, per, 1).astype(jnp.float32)
        for kk in range(K):
            grid = grid.at[:, base + cells[kk]].add(feats * values[kk][None, :])
        return grid

    grid = lax.fori_loop(0, parts, pool_one, jnp.zeros((C, cells_all), jnp.float32))
    pooled = grid.reshape(C, NX, NY, NZ).astype(jnp.bfloat16)
    kernel = conv_kernel.astype(jnp.float32)
    padded = jnp.pad(pooled.astype(jnp.float32), ((0, 0), (1, 1), (1, 1), (1, 1)))
    h_sum = jnp.zeros((C, NX, NY, NZ), jnp.float32)
    for oa in range(3):
        for ob in range(3):
            for oe in range(3):
                k = 9 * oa + 3 * ob + oe
                window = padded[:, oa:oa + NX, ob:ob + NY, oe:oe + NZ]
                h_sum = h_sum + jnp.einsum('io,ixyz->oxyz', kernel[k], window)
    latent = (pooled.astype(jnp.float32) + jax.nn.silu(h_sum)).astype(jnp.bfloat16)
    sig = jax.nn.sigmoid(h_sum)
    cot = cotangent.astype(jnp.float32)
    dh = (cot * sig * (1.0 + h_sum * (1.0 - sig))).astype(jnp.bfloat16)
    dh32 = dh.astype(jnp.float32)
    dpad = jnp.pad(dh32, ((0, 0), (1, 1), (1, 1), (1, 1)))
    dx = jnp.zeros((C, NX, NY, NZ), jnp.float32)
    kgrads = []
    for oa in range(3):
        for ob in range(3):
            for oe in range(3):
                k = 9 * oa + 3 * ob + oe
                back = dpad[:, 2 - oa:2 - oa + NX, 2 - ob:2 - ob + NY, 2 - oe:2 - oe + NZ]
                dx = dx + jnp.einsum('io,oxyz->ixyz', kernel[k], back)
                window = padded[:, oa:oa + NX, ob:ob + NY, oe:oe + NZ]
                kgrads.append(jnp.einsum('ixyz,oxyz->io', window, dh32))
    kernel_grad = jnp.stack(kgrads, 0) * jnp.float32(float(cells_all) ** -0.5)
    dpooled = (cot + dx).astype(jnp.bfloat16).reshape(C, cells_all).astype(jnp.float32)

    def grad_one(index, output):
        index = jnp.asarray(index).astype(jnp.int32)
        start, cells, base, values = partition_data(index, neighbour_cells, neighbour_weights, live_points, tile_target)
        total = jnp.zeros((C, per), jnp.float32)
        for kk in range(K):
            total = total + dpooled[:, base + cells[kk]] * values[kk][None, :]
        return lax.dynamic_update_slice_in_dim(output, total.astype(jnp.bfloat16), start, 1)

    feature_grad = lax.fori_loop(0, parts, grad_one, jnp.zeros((C, parts * per), jnp.bfloat16))
    return latent, feature_grad, kernel_grad
```

```python
import functools

import jax
import jax.numpy as jnp
from jax import lax
from jax.experimental import pallas as pl
from jax.experimental.pallas import tpu as pltpu
from jax.sharding import PartitionSpec as P

GROUP = 8
VMEM_LIMIT = 48 * 1024 * 1024


def pool_kernel(target, live, cells, weights, feats, blocks, send, acc):
    step = pl.program_id(0)
    tile = blocks.shape[2]
    depth = blocks.shape[1]

    @pl.when(step == 0)
    def _():
        acc[...] = jnp.zeros_like(acc)

    span = cells.shape[1]
    position = step * span + lax.broadcasted_iota(jnp.int32, cells.shape, 1)
    masked = jnp.where(position < live[0], weights[...], 0.0)
    cell = cells[...]
    depth_ids = lax.broadcasted_iota(jnp.int32, (depth, tile), 0)
    for t in range(span // tile):
        cols = slice(t * tile, (t + 1) * tile)
        total = jnp.zeros((depth, tile), jnp.float32)
        for k in range(cells.shape[0]):
            total = total + jnp.where(
                cell[k : k + 1, cols] == depth_ids, masked[k : k + 1, cols], 0.0
            )
        block = total.astype(jnp.bfloat16)
        blocks[t] = block
        part = lax.dot_general(
            feats[:, cols], block, (((1,), (1,)), ((), ())), preferred_element_type=jnp.float32
        )
        column = target[step * (span // tile) + t]
        acc[column] = acc[column] + part

    @pl.when(step == pl.num_programs(0) - 1)
    def _():
        send[...] = acc[...].astype(jnp.bfloat16)


def pool(target, live, cells, weights, feats, n_columns, depth):
    nbrs, npts = cells.shape
    half = feats.shape[0]
    tiles = target.shape[0]
    tile = npts // tiles
    group = min(GROUP, tiles)
    span = group * tile
    smem = pl.BlockSpec(memory_space=pltpu.SMEM)
    return pl.pallas_call(
        pool_kernel,
        grid=(tiles // group,),
        in_specs=[
            smem,
            smem,
            pl.BlockSpec((nbrs, span), lambda i: (0, i)),
            pl.BlockSpec((nbrs, span), lambda i: (0, i)),
            pl.BlockSpec((half, span), lambda i: (0, i)),
        ],
        out_specs=[
            pl.BlockSpec((group, depth, tile), lambda i: (i, 0, 0)),
            pl.BlockSpec((n_columns, half, depth), lambda i: (0, 0, 0)),
        ],
        out_shape=[
            jax.ShapeDtypeStruct((tiles, depth, tile), jnp.bfloat16),
            jax.ShapeDtypeStruct((n_columns, half, depth), jnp.bfloat16),
        ],
        scratch_shapes=[pltpu.VMEM((n_columns, half, depth), jnp.float32)],
        compiler_params=pltpu.CompilerParams(vmem_limit_bytes=VMEM_LIMIT),
        name="pool",
    )(target, live, cells, weights, feats)


def spread_kernel(target, columns, blocks, out):
    step = pl.program_id(0)
    group, _, tile = blocks.shape
    for t in range(group):
        column = target[step * group + t]
        part = jnp.dot(columns[column], blocks[t], preferred_element_type=jnp.float32)
        out[:, t * tile : (t + 1) * tile] = part.astype(jnp.bfloat16)


def spread(target, columns, blocks):
    tiles, depth, tile = blocks.shape
    n_columns, half, _ = columns.shape
    group = min(GROUP, tiles)
    return pl.pallas_call(
        spread_kernel,
        grid=(tiles // group,),
        in_specs=[
            pl.BlockSpec(memory_space=pltpu.SMEM),
            pl.BlockSpec((n_columns, half, depth), lambda i: (0, 0, 0)),
            pl.BlockSpec((group, depth, tile), lambda i: (i, 0, 0)),
        ],
        out_specs=pl.BlockSpec((half, group * tile), lambda i: (0, i)),
        out_shape=jax.ShapeDtypeStruct((half, tiles * tile), jnp.bfloat16),
        compiler_params=pltpu.CompilerParams(vmem_limit_bytes=VMEM_LIMIT),
        name="spread",
    )(target, columns, blocks)


def later(value, lane):
    return jnp.where(lane == 0, 0.0, pltpu.roll(value, 1, 1))


def earlier(value, lane):
    depth = value.shape[1]
    return jnp.where(lane == depth - 1, 0.0, pltpu.roll(value, depth - 1, 1))


def conv_kernel_body(chan, pooled, cot, wf, wb, latent, dpooled, kgrad, pp, dd, hh):
    half, depth = pooled.shape[4], pooled.shape[5]
    full = 2 * half
    first = pl.multiple_of(chan[0] * half, half)
    for s in range(3):
        for y in range(6):
            for x in range(2):
                for c in range(2):
                    pp[2 * s + x, y * full + c * half : y * full + (c + 1) * half, :] = pooled[
                        c, s, y, x
                    ]
    lane = lax.broadcasted_iota(jnp.int32, (full, depth), 1)
    for x in range(4):
        for y in range(4):
            grown = jnp.zeros((3 * full, depth), jnp.float32)
            for a in range(3):
                grown = grown + jnp.dot(
                    wf[a],
                    pp[x + a, y * full : (y + 3) * full, :],
                    preferred_element_type=jnp.float32,
                )
            h = (
                grown[full : 2 * full]
                + later(grown[:full], lane)
                + earlier(grown[2 * full :], lane)
            )
            sig = jax.nn.sigmoid(h)
            upper = jnp.concatenate([cot[0, y, x], cot[1, y, x]], 0).astype(jnp.float32)
            dd[x, y * full : (y + 1) * full, :] = (upper * sig * (1.0 + h * (1.0 - sig))).astype(
                jnp.bfloat16
            )
            if x in (1, 2) and y in (1, 2):
                hh[...] = h * sig
                mine = pp[x + 1, pl.ds((y + 1) * full + first, half), :].astype(jnp.float32)
                latent[:, x - 1, y - 1, :] = (mine + hh[pl.ds(first, half), :]).astype(jnp.bfloat16)
    lane = lax.broadcasted_iota(jnp.int32, (half, depth), 1)
    for x in range(2):
        for y in range(2):
            grown = jnp.zeros((3 * half, depth), jnp.float32)
            for a in range(3):
                grown = grown + jnp.dot(
                    wb[a],
                    dd[x + a, y * full : (y + 3) * full, :],
                    preferred_element_type=jnp.float32,
                )
            dx = (
                grown[half : 2 * half]
                + earlier(grown[:half], lane)
                + later(grown[2 * half :], lane)
            )
            own = cot[chan[0], y + 1, x + 1].astype(jnp.float32)
            dpooled[y, x] = (own + dx).astype(jnp.bfloat16)
    moved = []
    for x in range(2):
        for y in range(2):
            own = dd[x + 1, pl.ds((y + 1) * full + first, half), :].astype(jnp.float32)
            moved.append(
                jnp.concatenate(
                    [earlier(own, lane), own, later(own, lane), jnp.zeros_like(own)], 0
                ).astype(jnp.bfloat16)
            )
    for a in range(3):
        total = jnp.zeros((3 * full, 4 * half), jnp.float32)
        for x in range(2):
            for y in range(2):
                total = total + lax.dot_general(
                    pp[x + 1 + a, (y + 1) * full : (y + 4) * full, :],
                    moved[2 * x + y],
                    (((1,), (1,)), ((), ())),
                    preferred_element_type=jnp.float32,
                )
        kgrad[a * 3 * full : (a + 1) * 3 * full, :] = total.astype(jnp.bfloat16)
    rest = kgrad.shape[0] - 9 * full
    if rest:
        kgrad[9 * full :, :] = jnp.zeros((rest, 4 * half), jnp.bfloat16)


def conv_layer(chan, pooled, cot, wf, wb, rows):
    half, depth = pooled.shape[4], pooled.shape[5]
    full = 2 * half
    vmem = pl.BlockSpec(memory_space=pltpu.VMEM)
    return pl.pallas_call(
        conv_kernel_body,
        in_specs=[pl.BlockSpec(memory_space=pltpu.SMEM), vmem, vmem, vmem, vmem],
        out_specs=[vmem, vmem, vmem],
        out_shape=[
            jax.ShapeDtypeStruct((half, 2, 2, depth), jnp.bfloat16),
            jax.ShapeDtypeStruct((2, 2, half, depth), jnp.bfloat16),
            jax.ShapeDtypeStruct((rows, 4 * half), jnp.bfloat16),
        ],
        scratch_shapes=[
            pltpu.VMEM((6, 6 * full, depth), jnp.bfloat16),
            pltpu.VMEM((4, 4 * full, depth), jnp.bfloat16),
            pltpu.VMEM((full, depth), jnp.float32),
        ],
        compiler_params=pltpu.CompilerParams(vmem_limit_bytes=VMEM_LIMIT),
        name="conv_layer",
    )(chan, pooled, cot, wf, wb)


def neighbours(first, last, axis):
    peers = lax.axis_size(axis)
    up = [(i, i + 1) for i in range(peers - 1)]
    down = [(j, i) for i, j in up]
    return lax.ppermute(last, axis, up), lax.ppermute(first, axis, down)


def body(
    point_features,
    neighbour_cells,
    neighbour_weights,
    live_points,
    tile_target,
    conv_kernel,
    cotangent,
):
    half = point_features.shape[0]
    full = 2 * half
    xsize, ysize, depth = cotangent.shape[1:]
    n_dom, n_slab = lax.axis_size("dom"), lax.axis_size("slab")
    devices = n_dom * n_slab
    width = xsize * ysize
    chan = lax.axis_index("chan").astype(jnp.int32)
    scale = float(width * depth * devices) ** (-0.5)

    blocks, send = pool(
        tile_target,
        live_points,
        neighbour_cells,
        neighbour_weights,
        point_features,
        n_dom * width,
        depth,
    )

    cot = cotangent.transpose(2, 1, 0, 3)
    before, after = neighbours(cot[:1], cot[-1:], "dom")
    cot = jnp.concatenate([before, cot, after], 0)
    before, after = neighbours(cot[:, :1], cot[:, -1:], "slab")
    cot = jnp.concatenate([before, cot, after], 1)
    cot = lax.all_gather(cot, "chan", axis=0, tiled=False)

    kernel = conv_kernel.reshape(3, 3, 3, full, full)
    wf = kernel.transpose(0, 2, 4, 1, 3).reshape(3, 3 * full, 3 * full)
    wb = lax.dynamic_slice_in_dim(kernel[::-1, ::-1], chan * half, half, 3)
    wb = wb.transpose(0, 2, 3, 1, 4).reshape(3, 3 * half, 3 * full)

    recv = lax.all_to_all(send, "dom", split_axis=0, concat_axis=0, tiled=True)
    pooled = recv.reshape(n_dom, ysize, xsize, half, depth).astype(jnp.float32).sum(0)
    pooled = pooled.astype(jnp.bfloat16)
    before, after = neighbours(pooled, pooled, "dom")
    pooled = jnp.concatenate([before, pooled, after], 0)
    before, after = neighbours(pooled, pooled, "slab")
    pooled = jnp.stack([before, pooled, after], 0)
    pooled = lax.all_gather(pooled, "chan", axis=0, tiled=False)

    per = -(-9 * full // (4 * devices)) * 4
    latent, dpooled, kgrad = conv_layer(chan[None], pooled, cot, wf, wb, per * devices)

    columns = jnp.broadcast_to(dpooled.reshape(1, width, half, depth), (n_dom, width, half, depth))
    columns = lax.all_to_all(
        columns.reshape(n_dom * width, half, depth), "dom", split_axis=0, concat_axis=0, tiled=True
    )
    feature_grad = spread(tile_target, columns, blocks)

    kgrad = lax.all_to_all(
        kgrad.reshape(devices, per, 4 * half), ("dom", "slab"), split_axis=0, concat_axis=0, tiled=True
    )
    kgrad = (kgrad.astype(jnp.float32).sum(0) * scale).astype(jnp.bfloat16)
    kgrad = jnp.broadcast_to(kgrad[None], (2 * devices, per, 4 * half))
    kgrad = lax.all_to_all(kgrad, ("dom", "slab", "chan"), split_axis=0, concat_axis=0, tiled=True)
    kgrad = kgrad.reshape(devices, 2, per, 4 * half).transpose(0, 2, 1, 3)
    kgrad = kgrad.reshape(devices * per, 2, 4 * half)[: 9 * full, :, : 3 * half]
    kgrad = kgrad.reshape(9, full, 2, 3, half).transpose(0, 3, 1, 2, 4)
    kernel_grad = kgrad.reshape(27, full, full).astype(jnp.float32)
    return (latent, feature_grad, kernel_grad)


def solution(mesh):
    placed = (
        P("chan", ("dom", "slab")),
        P(None, ("dom", "slab")),
        P(None, ("dom", "slab")),
        P(("dom", "slab")),
        P(("dom", "slab")),
        P(),
        P("chan", "slab", "dom", None),
    )
    return jax.shard_map(
        body,
        mesh=mesh,
        in_specs=placed,
        out_specs=(P("chan", "slab", "dom", None), P("chan", ("dom", "slab")), P()),
        check_vma=False,
    )
```

```python
import functools

import jax
import jax.numpy as jnp
from jax import lax
from jax.experimental import pallas as pl
from jax.experimental.pallas import tpu as pltpu
from jax.sharding import PartitionSpec as P

GROUP = 8
POOL_VMEM = 60 * 1024 * 1024
VMEM_LIMIT = 16 * 1024 * 1024
CHUNK = 16


def cost(flops, moved):
    return pl.CostEstimate(flops=flops, bytes_accessed=moved, transcendentals=0)


def pool_kernel(target, live, cells, weights, feats, blocks, send, acc):
    step = pl.program_id(0)
    tile = blocks.shape[2]
    depth = blocks.shape[1]

    @pl.when(step == 0)
    def _():
        acc[...] = jnp.zeros_like(acc)

    span = cells.shape[1]
    position = step * span + lax.broadcasted_iota(jnp.int32, cells.shape, 1)
    masked = jnp.where(position < live[0], weights[...], 0.0)
    cell = cells[...]
    depth_ids = lax.broadcasted_iota(jnp.int32, (depth, tile), 0)
    for t in range(span // tile):
        cols = slice(t * tile, (t + 1) * tile)
        total = jnp.zeros((depth, tile), jnp.float32)
        for k in range(cells.shape[0]):
            total = total + jnp.where(
                cell[k : k + 1, cols] == depth_ids, masked[k : k + 1, cols], 0.0
            )
        block = total.astype(jnp.bfloat16)
        blocks[t] = block
        part = lax.dot_general(
            feats[:, cols], block, (((1,), (1,)), ((), ())), preferred_element_type=jnp.float32
        )
        column = target[step * (span // tile) + t]
        acc[column] = acc[column] + part

    @pl.when(step == pl.num_programs(0) - 1)
    def _():
        send[...] = acc[...].astype(jnp.bfloat16)


def pool(target, live, cells, weights, feats, n_columns, depth):
    nbrs, npts = cells.shape
    half = feats.shape[0]
    tiles = target.shape[0]
    tile = npts // tiles
    group = min(GROUP, tiles)
    span = group * tile
    smem = pl.BlockSpec(memory_space=pltpu.SMEM)
    return pl.pallas_call(
        pool_kernel,
        grid=(tiles // group,),
        in_specs=[
            smem,
            smem,
            pl.BlockSpec((nbrs, span), lambda i: (0, i)),
            pl.BlockSpec((nbrs, span), lambda i: (0, i)),
            pl.BlockSpec((half, span), lambda i: (0, i)),
        ],
        out_specs=[
            pl.BlockSpec((group, depth, tile), lambda i: (i, 0, 0)),
            pl.BlockSpec((n_columns, half, depth), lambda i: (0, 0, 0)),
        ],
        out_shape=[
            jax.ShapeDtypeStruct((tiles, depth, tile), jnp.bfloat16),
            jax.ShapeDtypeStruct((n_columns, half, depth), jnp.bfloat16),
        ],
        scratch_shapes=[pltpu.VMEM((n_columns, half, depth), jnp.float32)],
        compiler_params=pltpu.CompilerParams(vmem_limit_bytes=POOL_VMEM),
        cost_estimate=cost(2 * half * npts * depth, 24 * nbrs * npts * depth // 8),
        name="pool",
    )(target, live, cells, weights, feats)


def spread_kernel(target, columns, blocks, out):
    step = pl.program_id(0)
    group, _, tile = blocks.shape
    half = out.shape[0]
    for t in range(group):
        column = target[step * group + t]
        first = pl.multiple_of(column % 4 * half, half)
        own = columns[column // 4, pl.ds(first, half), :]
        part = jnp.dot(own, blocks[t], preferred_element_type=jnp.float32)
        out[:, t * tile : (t + 1) * tile] = part.astype(jnp.bfloat16)


def spread(target, columns, blocks, half):
    tiles, depth, tile = blocks.shape
    group = min(GROUP, tiles)
    return pl.pallas_call(
        spread_kernel,
        grid=(tiles // group,),
        in_specs=[
            pl.BlockSpec(memory_space=pltpu.SMEM),
            pl.BlockSpec(columns.shape, lambda i: (0, 0, 0)),
            pl.BlockSpec((group, depth, tile), lambda i: (i, 0, 0)),
        ],
        out_specs=pl.BlockSpec((half, group * tile), lambda i: (0, i)),
        out_shape=jax.ShapeDtypeStruct((half, tiles * tile), jnp.bfloat16),
        compiler_params=pltpu.CompilerParams(vmem_limit_bytes=VMEM_LIMIT),
        cost_estimate=cost(2 * half * tiles * tile * depth, 6 * tiles * tile * depth),
        name="spread",
    )(target, columns, blocks)


def unpack_kernel(gathered, out):
    half = out.shape[2] // 2
    per = gathered.shape[2] // CHUNK
    for k in range(out.shape[0]):
        rows = slice(k % per * CHUNK, (k % per + 1) * CHUNK)
        first = gathered[k // per, 0, rows, :].astype(jnp.float32)
        second = gathered[k // per, 1, rows, :].astype(jnp.float32)
        for g in range(out.shape[1] // CHUNK):
            lanes = slice(g * half, (g + 1) * half)
            out[k, g * CHUNK : (g + 1) * CHUNK, :] = jnp.concatenate(
                [first[:, lanes], second[:, lanes]], 1
            )


def unpack(gathered, offsets, full):
    vmem = pl.BlockSpec(memory_space=pltpu.VMEM)
    return pl.pallas_call(
        unpack_kernel,
        in_specs=[vmem],
        out_specs=vmem,
        out_shape=jax.ShapeDtypeStruct((offsets, full, full), jnp.float32),
        compiler_params=pltpu.CompilerParams(vmem_limit_bytes=VMEM_LIMIT),
        name="unpack",
    )(gathered)


def later(value, lane):
    return jnp.where(lane == 0, 0.0, pltpu.roll(value, 1, 1))


def earlier(value, lane):
    depth = value.shape[1]
    return jnp.where(lane == depth - 1, 0.0, pltpu.roll(value, depth - 1, 1))


def conv_kernel_body(chan, pooled, cot, wf, wb, latent, message, pp, dd, hh):
    half, depth = pooled.shape[4], pooled.shape[5]
    full = 2 * half
    n_dom = message.shape[0]
    per = message.shape[1] // CHUNK - 4 * half // CHUNK
    first = pl.multiple_of(chan[0] * half, half)
    for s in range(3):
        for y in range(6):
            for x in range(2):
                for c in range(2):
                    pp[2 * s + x, y * full + c * half : y * full + (c + 1) * half, :] = pooled[
                        c, s, y, x
                    ]
    lane = lax.broadcasted_iota(jnp.int32, (full, depth), 1)
    for x in range(4):
        for y in range(4):
            grown = jnp.zeros((3 * full, depth), jnp.float32)
            for a in range(3):
                grown = grown + jnp.dot(
                    wf[a],
                    pp[x + a, y * full : (y + 3) * full, :],
                    preferred_element_type=jnp.float32,
                )
            h = (
                grown[full : 2 * full]
                + later(grown[:full], lane)
                + earlier(grown[2 * full :], lane)
            )
            sig = jax.nn.sigmoid(h)
            upper = jnp.concatenate([cot[0, y, x], cot[1, y, x]], 0).astype(jnp.float32)
            dd[x, y * full : (y + 1) * full, :] = (upper * sig * (1.0 + h * (1.0 - sig))).astype(
                jnp.bfloat16
            )
            if x in (1, 2) and y in (1, 2):
                hh[...] = h * sig
                mine = pp[x + 1, pl.ds((y + 1) * full + first, half), :].astype(jnp.float32)
                latent[:, x - 1, y - 1, :] = (mine + hh[pl.ds(first, half), :]).astype(jnp.bfloat16)
    lane = lax.broadcasted_iota(jnp.int32, (half, depth), 1)
    for x in range(2):
        for y in range(2):
            grown = jnp.zeros((3 * half, depth), jnp.float32)
            for a in range(3):
                grown = grown + jnp.dot(
                    wb[a],
                    dd[x + a, y * full : (y + 3) * full, :],
                    preferred_element_type=jnp.float32,
                )
            dx = (
                grown[half : 2 * half]
                + earlier(grown[:half], lane)
                + later(grown[2 * half :], lane)
            )
            own = cot[chan[0], y + 1, x + 1].astype(jnp.float32)
            column = (own + dx).astype(jnp.bfloat16)
            for d in range(n_dom):
                message[d, (2 * y + x) * half : (2 * y + x + 1) * half, :] = column
    moved = []
    for x in range(2):
        for y in range(2):
            own = dd[x + 1, pl.ds((y + 1) * full + first, half), :].astype(jnp.float32)
            moved.append(
                jnp.concatenate(
                    [earlier(own, lane), own, later(own, lane), jnp.zeros_like(own)], 0
                ).astype(jnp.bfloat16)
            )
    for a in range(3):
        total = jnp.zeros((3 * full, 4 * half), jnp.float32)
        for x in range(2):
            for y in range(2):
                total = total + lax.dot_general(
                    pp[x + 1 + a, (y + 1) * full : (y + 4) * full, :],
                    moved[2 * x + y],
                    (((1,), (1,)), ((), ())),
                    preferred_element_type=jnp.float32,
                )
        for b in range(3):
            for e in range(3):
                k = 9 * a + 3 * b + e
                pieces = [
                    total[b * full + g * CHUNK : b * full + (g + 1) * CHUNK, e * half : (e + 1) * half]
                    for g in range(full // CHUNK)
                ]
                row = 4 * half + k % per * CHUNK
                message[k // per, row : row + CHUNK, :] = jnp.concatenate(pieces, 1).astype(
                    jnp.bfloat16
                )
    for k in range(27, n_dom * per):
        row = 4 * half + k % per * CHUNK
        message[k // per, row : row + CHUNK, :] = jnp.zeros((CHUNK, depth), jnp.bfloat16)


def conv_layer(chan, pooled, cot, wf, wb, n_dom):
    half, depth = pooled.shape[4], pooled.shape[5]
    full = 2 * half
    per = -(-27 // n_dom)
    vmem = pl.BlockSpec(memory_space=pltpu.VMEM)
    return pl.pallas_call(
        conv_kernel_body,
        in_specs=[pl.BlockSpec(memory_space=pltpu.SMEM), vmem, vmem, vmem, vmem],
        out_specs=[vmem, vmem],
        out_shape=[
            jax.ShapeDtypeStruct((half, 2, 2, depth), jnp.bfloat16),
            jax.ShapeDtypeStruct((n_dom, 4 * half + per * CHUNK, depth), jnp.bfloat16),
        ],
        scratch_shapes=[
            pltpu.VMEM((6, 6 * full, depth), jnp.bfloat16),
            pltpu.VMEM((4, 4 * full, depth), jnp.bfloat16),
            pltpu.VMEM((full, depth), jnp.float32),
        ],
        compiler_params=pltpu.CompilerParams(vmem_limit_bytes=VMEM_LIMIT),
        name="conv_layer",
    )(chan, pooled, cot, wf, wb)


def neighbours(first, last, axis):
    peers = lax.axis_size(axis)
    up = [(i, i + 1) for i in range(peers - 1)]
    down = [(j, i) for i, j in up]
    return lax.ppermute(last, axis, up), lax.ppermute(first, axis, down)


def body(
    point_features,
    neighbour_cells,
    neighbour_weights,
    live_points,
    tile_target,
    conv_kernel,
    cotangent,
):
    half = point_features.shape[0]
    full = 2 * half
    xsize, ysize, depth = cotangent.shape[1:]
    n_dom, n_slab = lax.axis_size("dom"), lax.axis_size("slab")
    width = xsize * ysize
    chan = lax.axis_index("chan").astype(jnp.int32)
    scale = float(width * depth * n_dom * n_slab) ** (-0.5)

    blocks, send = pool(
        tile_target,
        live_points,
        neighbour_cells,
        neighbour_weights,
        point_features,
        n_dom * width,
        depth,
    )

    cot = cotangent.transpose(2, 1, 0, 3)
    before, after = neighbours(cot[:1], cot[-1:], "dom")
    cot = jnp.concatenate([before, cot, after], 0)
    send, cot = lax.optimization_barrier((send, cot))
    before, after = neighbours(cot[:, :1], cot[:, -1:], "slab")
    cot = jnp.concatenate([before, cot, after], 1)
    cot = lax.all_gather(cot, "chan", axis=0, tiled=False)

    kernel = conv_kernel.reshape(3, 3, 3, full, full)
    wf = kernel.transpose(0, 2, 4, 1, 3).reshape(3, 3 * full, 3 * full)
    wb = lax.dynamic_slice_in_dim(kernel[::-1, ::-1], chan * half, half, 3)
    wb = wb.transpose(0, 2, 3, 1, 4).reshape(3, 3 * half, 3 * full)

    recv = lax.all_to_all(send, "dom", split_axis=0, concat_axis=0, tiled=True)
    recv, cot, wf, wb = lax.optimization_barrier((recv, cot, wf, wb))
    pooled = recv.reshape(n_dom, ysize, xsize, half, depth).astype(jnp.float32).sum(0)
    pooled = pooled.astype(jnp.bfloat16)
    before, after = neighbours(pooled, pooled, "dom")
    pooled = jnp.concatenate([before, pooled, after], 0)
    before, after = neighbours(pooled, pooled, "slab")
    pooled = jnp.stack([before, pooled, after], 0)
    pooled = lax.all_gather(pooled, "chan", axis=0, tiled=False)

    latent, message = conv_layer(chan[None], pooled, cot, wf, wb, n_dom)
    columns = lax.all_to_all(message, "dom", split_axis=0, concat_axis=0, tiled=True)
    kgrad = columns[:, width * half :].astype(jnp.float32).sum(0).astype(jnp.bfloat16)
    kgrad = jnp.broadcast_to(kgrad[None], (2 * n_slab,) + kgrad.shape)
    kgrad = lax.all_to_all(kgrad, ("slab", "chan"), split_axis=0, concat_axis=0, tiled=True)
    feature_grad = spread(tile_target, columns, blocks, half)
    kgrad = kgrad.reshape((n_slab, 2) + kgrad.shape[1:]).astype(jnp.float32).sum(0) * scale
    kgrad = jnp.broadcast_to(kgrad.astype(jnp.bfloat16)[None], (n_dom,) + kgrad.shape)
    kgrad = lax.all_to_all(kgrad, "dom", split_axis=0, concat_axis=0, tiled=True)
    kernel_grad = unpack(kgrad, 27, full)
    return (latent, feature_grad, kernel_grad)


def solution(mesh):
    placed = (
        P("chan", ("dom", "slab")),
        P(None, ("dom", "slab")),
        P(None, ("dom", "slab")),
        P(("dom", "slab")),
        P(("dom", "slab")),
        P(),
        P("chan", "slab", "dom", None),
    )
    return jax.shard_map(
        body,
        mesh=mesh,
        in_specs=placed,
        out_specs=(P("chan", "slab", "dom", None), P("chan", ("dom", "slab")), P()),
        check_vma=False,
    )
```

```python
import functools

import jax
import jax.numpy as jnp
from jax import lax
from jax.experimental import pallas as pl
from jax.experimental.pallas import tpu as pltpu
from jax.sharding import PartitionSpec as P

GROUP = 8
POOL_VMEM = 60 * 1024 * 1024
VMEM_LIMIT = 16 * 1024 * 1024
CHUNK = 16


def cost(flops, moved):
    return pl.CostEstimate(flops=flops, bytes_accessed=moved, transcendentals=0)


def pool_kernel(target, live, cells, weights, feats, blocks, send, acc):
    step = pl.program_id(0)
    tile = blocks.shape[2]
    depth = blocks.shape[1]

    @pl.when(step == 0)
    def _():
        acc[...] = jnp.zeros_like(acc)

    span = cells.shape[1]
    position = step * span + lax.broadcasted_iota(jnp.int32, cells.shape, 1)
    masked = jnp.where(position < live[0], weights[...], 0.0)
    cell = cells[...]
    depth_ids = lax.broadcasted_iota(jnp.int32, (depth, tile), 0)
    for t in range(span // tile):
        cols = slice(t * tile, (t + 1) * tile)
        total = jnp.zeros((depth, tile), jnp.float32)
        for k in range(cells.shape[0]):
            total = total + jnp.where(
                cell[k : k + 1, cols] == depth_ids, masked[k : k + 1, cols], 0.0
            )
        block = total.astype(jnp.bfloat16)
        blocks[t] = block
        part = lax.dot_general(
            feats[:, cols], block, (((1,), (1,)), ((), ())), preferred_element_type=jnp.float32
        )
        column = target[step * (span // tile) + t]
        acc[column] = acc[column] + part

    @pl.when(step == pl.num_programs(0) - 1)
    def _():
        send[...] = acc[...].astype(jnp.bfloat16)


def pool(target, live, cells, weights, feats, n_columns, depth):
    nbrs, npts = cells.shape
    half = feats.shape[0]
    tiles = target.shape[0]
    tile = npts // tiles
    group = min(GROUP, tiles)
    span = group * tile
    smem = pl.BlockSpec(memory_space=pltpu.SMEM)
    return pl.pallas_call(
        pool_kernel,
        grid=(tiles // group,),
        in_specs=[
            smem,
            smem,
            pl.BlockSpec((nbrs, span), lambda i: (0, i)),
            pl.BlockSpec((nbrs, span), lambda i: (0, i)),
            pl.BlockSpec((half, span), lambda i: (0, i)),
        ],
        out_specs=[
            pl.BlockSpec((group, depth, tile), lambda i: (i, 0, 0)),
            pl.BlockSpec((n_columns, half, depth), lambda i: (0, 0, 0)),
        ],
        out_shape=[
            jax.ShapeDtypeStruct((tiles, depth, tile), jnp.bfloat16),
            jax.ShapeDtypeStruct((n_columns, half, depth), jnp.bfloat16),
        ],
        scratch_shapes=[pltpu.VMEM((n_columns, half, depth), jnp.float32)],
        compiler_params=pltpu.CompilerParams(vmem_limit_bytes=POOL_VMEM),
        cost_estimate=cost(2 * half * npts * depth, 24 * nbrs * npts * depth // 8),
        name="pool",
    )(target, live, cells, weights, feats)


def spread_kernel(inner, target, columns, blocks, out):
    step = pl.program_id(0)
    group, _, tile = blocks.shape
    half = out.shape[0]
    for t in range(group):
        column = target[step * group + t]
        first = pl.multiple_of(column % inner * half, half)
        own = columns[column // inner, pl.ds(first, half), :]
        part = jnp.dot(own, blocks[t], preferred_element_type=jnp.float32)
        out[:, t * tile : (t + 1) * tile] = part.astype(jnp.bfloat16)


def spread(target, columns, blocks, half, inner):
    tiles, depth, tile = blocks.shape
    group = min(GROUP, tiles)
    return pl.pallas_call(
        functools.partial(spread_kernel, inner),
        grid=(tiles // group,),
        in_specs=[
            pl.BlockSpec(memory_space=pltpu.SMEM),
            pl.BlockSpec(columns.shape, lambda i: (0, 0, 0)),
            pl.BlockSpec((group, depth, tile), lambda i: (i, 0, 0)),
        ],
        out_specs=pl.BlockSpec((half, group * tile), lambda i: (0, i)),
        out_shape=jax.ShapeDtypeStruct((half, tiles * tile), jnp.bfloat16),
        compiler_params=pltpu.CompilerParams(vmem_limit_bytes=VMEM_LIMIT),
        cost_estimate=cost(2 * half * tiles * tile * depth, 6 * tiles * tile * depth),
        name="spread",
    )(target, columns, blocks)


def unpack_kernel(gathered, out):
    half = out.shape[2] // 2
    per = gathered.shape[2] // CHUNK
    for k in range(out.shape[0]):
        rows = slice(k % per * CHUNK, (k % per + 1) * CHUNK)
        first = gathered[k // per, 0, rows, :].astype(jnp.float32)
        second = gathered[k // per, 1, rows, :].astype(jnp.float32)
        for g in range(out.shape[1] // CHUNK):
            lanes = slice(g * half, (g + 1) * half)
            out[k, g * CHUNK : (g + 1) * CHUNK, :] = jnp.concatenate(
                [first[:, lanes], second[:, lanes]], 1
            )


def unpack(gathered, offsets, full):
    vmem = pl.BlockSpec(memory_space=pltpu.VMEM)
    return pl.pallas_call(
        unpack_kernel,
        in_specs=[vmem],
        out_specs=vmem,
        out_shape=jax.ShapeDtypeStruct((offsets, full, full), jnp.float32),
        compiler_params=pltpu.CompilerParams(vmem_limit_bytes=VMEM_LIMIT),
        name="unpack",
    )(gathered)


def later(value, lane):
    return jnp.where(lane == 0, 0.0, pltpu.roll(value, 1, 1))


def earlier(value, lane):
    depth = value.shape[1]
    return jnp.where(lane == depth - 1, 0.0, pltpu.roll(value, depth - 1, 1))


def conv_kernel_body(chan, grid, wf, wb, latent, message, pp, dd, hh):
    half, depth = grid.shape[2], grid.shape[3]
    full = 2 * half
    n_dom = message.shape[0]

    def cot(c, y, x):
        return grid[c, (12 + y, 27 + 2 * y + x, 27 + 2 * y + x, 48 + y)[x]]

    per = message.shape[1] // CHUNK - 4 * half // CHUNK
    first = pl.multiple_of(chan[0] * half, half)
    for s in range(3):
        for y in range(6):
            for x in range(2):
                for c in range(2):
                    rows = slice(y * full + c * half, y * full + (c + 1) * half)
                    pp[2 * s + x, rows, :] = grid[c, (0, 16, 36)[s] + 2 * y + x]
    lane = lax.broadcasted_iota(jnp.int32, (full, depth), 1)
    for x in range(4):
        for y in range(4):
            grown = jnp.zeros((3 * full, depth), jnp.float32)
            for a in range(3):
                grown = grown + jnp.dot(
                    wf[a],
                    pp[x + a, y * full : (y + 3) * full, :],
                    preferred_element_type=jnp.float32,
                )
            h = (
                grown[full : 2 * full]
                + later(grown[:full], lane)
                + earlier(grown[2 * full :], lane)
            )
            sig = jax.nn.sigmoid(h)
            upper = jnp.concatenate([cot(0, y, x), cot(1, y, x)], 0).astype(jnp.float32)
            dd[x, y * full : (y + 1) * full, :] = (upper * sig * (1.0 + h * (1.0 - sig))).astype(
                jnp.bfloat16
            )
            if x in (1, 2) and y in (1, 2):
                hh[...] = h * sig
                mine = pp[x + 1, pl.ds((y + 1) * full + first, half), :].astype(jnp.float32)
                latent[:, x - 1, y - 1, :] = (mine + hh[pl.ds(first, half), :]).astype(jnp.bfloat16)
    lane = lax.broadcasted_iota(jnp.int32, (half, depth), 1)
    for x in range(2):
        for y in range(2):
            grown = jnp.zeros((3 * half, depth), jnp.float32)
            for a in range(3):
                grown = grown + jnp.dot(
                    wb[a],
                    dd[x + a, y * full : (y + 3) * full, :],
                    preferred_element_type=jnp.float32,
                )
            dx = (
                grown[half : 2 * half]
                + earlier(grown[:half], lane)
                + later(grown[2 * half :], lane)
            )
            own = cot(chan[0], y + 1, x + 1).astype(jnp.float32)
            column = (own + dx).astype(jnp.bfloat16)
            for d in range(n_dom):
                message[d, (2 * y + x) * half : (2 * y + x + 1) * half, :] = column
    moved = []
    for x in range(2):
        for y in range(2):
            own = dd[x + 1, pl.ds((y + 1) * full + first, half), :].astype(jnp.float32)
            moved.append(
                jnp.concatenate(
                    [earlier(own, lane), own, later(own, lane), jnp.zeros_like(own)], 0
                ).astype(jnp.bfloat16)
            )
    for a in range(3):
        total = jnp.zeros((3 * full, 4 * half), jnp.float32)
        for x in range(2):
            for y in range(2):
                total = total + lax.dot_general(
                    pp[x + 1 + a, (y + 1) * full : (y + 4) * full, :],
                    moved[2 * x + y],
                    (((1,), (1,)), ((), ())),
                    preferred_element_type=jnp.float32,
                )
        for b in range(3):
            for e in range(3):
                k = 9 * a + 3 * b + e
                pieces = [
                    total[b * full + g * CHUNK : b * full + (g + 1) * CHUNK, e * half : (e + 1) * half]
                    for g in range(full // CHUNK)
                ]
                row = 4 * half + k % per * CHUNK
                message[k // per, row : row + CHUNK, :] = jnp.concatenate(pieces, 1).astype(
                    jnp.bfloat16
                )
    for k in range(27, n_dom * per):
        row = 4 * half + k % per * CHUNK
        message[k // per, row : row + CHUNK, :] = jnp.zeros((CHUNK, depth), jnp.bfloat16)


def conv_layer(chan, grid, wf, wb, n_dom):
    half, depth = grid.shape[2], grid.shape[3]
    full = 2 * half
    per = -(-27 // n_dom)
    vmem = pl.BlockSpec(memory_space=pltpu.VMEM)
    return pl.pallas_call(
        conv_kernel_body,
        in_specs=[pl.BlockSpec(memory_space=pltpu.SMEM), vmem, vmem, vmem],
        out_specs=[vmem, vmem],
        out_shape=[
            jax.ShapeDtypeStruct((half, 2, 2, depth), jnp.bfloat16),
            jax.ShapeDtypeStruct((n_dom, 4 * half + per * CHUNK, depth), jnp.bfloat16),
        ],
        scratch_shapes=[
            pltpu.VMEM((6, 6 * full, depth), jnp.bfloat16),
            pltpu.VMEM((4, 4 * full, depth), jnp.bfloat16),
            pltpu.VMEM((full, depth), jnp.float32),
        ],
        compiler_params=pltpu.CompilerParams(vmem_limit_bytes=VMEM_LIMIT),
        name="conv_layer",
    )(chan, grid, wf, wb)


def relay_kernel(own, received, message):
    sources = received.shape[0]
    outer = message.shape[0]
    total = received[0, own:, :].astype(jnp.float32)
    for z in range(1, sources):
        total = total + received[z, own:, :].astype(jnp.float32)
    total = total.astype(jnp.bfloat16)
    for x in range(outer):
        for z in range(sources):
            message[x, z * own : (z + 1) * own, :] = received[z, :own, :]
        message[x, sources * own :, :] = total


def relay(received, outer, own):
    sources, rows, depth = received.shape
    vmem = pl.BlockSpec(memory_space=pltpu.VMEM)
    return pl.pallas_call(
        functools.partial(relay_kernel, own),
        in_specs=[vmem],
        out_specs=vmem,
        out_shape=jax.ShapeDtypeStruct((outer, sources * own + rows - own, depth), jnp.bfloat16),
        compiler_params=pltpu.CompilerParams(vmem_limit_bytes=VMEM_LIMIT),
        name="relay",
    )(received)


def neighbours(first, last, axis):
    peers = lax.axis_size(axis)
    up = [(i, i + 1) for i in range(peers - 1)]
    down = [(j, i) for i, j in up]
    return lax.ppermute(last, axis, up), lax.ppermute(first, axis, down)


def body(
    point_features,
    neighbour_cells,
    neighbour_weights,
    live_points,
    tile_target,
    conv_kernel,
    cotangent,
):
    half = point_features.shape[0]
    full = 2 * half
    xsize, ysize, depth = cotangent.shape[1:]
    n_dom, n_slab = lax.axis_size("dom"), lax.axis_size("slab")
    width = xsize * ysize
    chan = lax.axis_index("chan").astype(jnp.int32)
    scale = float(width * depth * n_dom * n_slab) ** (-0.5)

    blocks, send = pool(
        tile_target,
        live_points,
        neighbour_cells,
        neighbour_weights,
        point_features,
        n_dom * width,
        depth,
    )

    kernel = conv_kernel.reshape(3, 3, 3, full, full)
    wf = kernel.transpose(0, 2, 4, 1, 3).reshape(3, 3 * full, 3 * full)
    wb = lax.dynamic_slice_in_dim(kernel[::-1, ::-1], chan * half, half, 3)
    wb = wb.transpose(0, 2, 3, 1, 4).reshape(3, 3 * half, 3 * full)

    inner = min(8, n_dom // 2)
    outer = n_dom // inner
    same_z = [[x * inner + z for x in range(outer)] for z in range(inner)]
    same_x = [[x * inner + z for z in range(inner)] for x in range(outer)]

    def exchange(value, axis, groups=None):
        return lax.all_to_all(
            value, axis, split_axis=0, concat_axis=0, tiled=True, axis_index_groups=groups
        )

    def total(value, parts):
        return value.reshape((parts, -1) + value.shape[1:]).astype(jnp.float32).sum(0)

    part = total(exchange(send, "dom", same_z), outer).astype(jnp.bfloat16)
    part = exchange(part, "dom", same_x)
    part, wf, wb = lax.optimization_barrier((part, wf, wb))
    pooled = total(part, inner).astype(jnp.bfloat16)

    cot = cotangent.transpose(2, 1, 0, 3)
    before, after = neighbours(
        jnp.concatenate([pooled, cot[0]], 0), jnp.concatenate([pooled, cot[-1]], 0), "dom"
    )
    pooled = jnp.concatenate([before[:width], pooled, after[:width]], 0)
    cot = jnp.concatenate([before[None, width:], cot, after[None, width:]], 0)
    before, after = neighbours(
        jnp.concatenate([pooled, cot[:, 0]], 0), jnp.concatenate([pooled, cot[:, -1]], 0), "slab"
    )
    grid = jnp.concatenate([before, pooled, cot.reshape((-1,) + cot.shape[2:]), after], 0)
    grid = lax.all_gather(grid, "chan", axis=0, tiled=False)

    latent, message = conv_layer(chan[None], grid, wf, wb, inner)
    message = relay(exchange(message, "dom", same_x), outer, width * half)
    columns = exchange(message, "dom", same_z)
    kgrad = columns[:, inner * width * half :].astype(jnp.float32).sum(0).astype(jnp.bfloat16)
    kgrad = exchange(jnp.broadcast_to(kgrad[None], (2 * n_slab,) + kgrad.shape), ("slab", "chan"))
    feature_grad = spread(tile_target, columns, blocks, half, inner * width)
    kgrad = (total(kgrad, n_slab) * scale).astype(jnp.bfloat16)
    kgrad = exchange(jnp.broadcast_to(kgrad[None], (inner,) + kgrad.shape), "dom", same_x)
    kernel_grad = unpack(kgrad, 27, full)
    return (latent, feature_grad, kernel_grad)


def solution(mesh):
    placed = (
        P("chan", ("dom", "slab")),
        P(None, ("dom", "slab")),
        P(None, ("dom", "slab")),
        P(("dom", "slab")),
        P(("dom", "slab")),
        P(),
        P("chan", "slab", "dom", None),
    )
    return jax.shard_map(
        body,
        mesh=mesh,
        in_specs=placed,
        out_specs=(P("chan", "slab", "dom", None), P("chan", ("dom", "slab")), P()),
        check_vma=False,
    )
```

```python
import functools

import jax
import jax.numpy as jnp
from jax import lax
from jax.experimental import pallas as pl
from jax.experimental.pallas import tpu as pltpu
from jax.sharding import PartitionSpec as P

GROUP = 8
POOL_VMEM = 60 * 1024 * 1024
VMEM_LIMIT = 16 * 1024 * 1024
CHUNK = 16


def cost(flops, moved):
    return pl.CostEstimate(flops=flops, bytes_accessed=moved, transcendentals=0)


def pool_kernel(target, live, cells, weights, feats, blocks, send, acc):
    step = pl.program_id(0)
    tile = blocks.shape[2]
    depth = blocks.shape[1]

    @pl.when(step == 0)
    def _():
        acc[...] = jnp.zeros_like(acc)

    span = cells.shape[1]
    position = step * span + lax.broadcasted_iota(jnp.int32, cells.shape, 1)
    masked = jnp.where(position < live[0], weights[...], 0.0)
    cell = cells[...]
    depth_ids = lax.broadcasted_iota(jnp.int32, (depth, tile), 0)
    for t in range(span // tile):
        cols = slice(t * tile, (t + 1) * tile)
        total = jnp.zeros((depth, tile), jnp.float32)
        for k in range(cells.shape[0]):
            total = total + jnp.where(
                cell[k : k + 1, cols] == depth_ids, masked[k : k + 1, cols], 0.0
            )
        block = total.astype(jnp.bfloat16)
        blocks[t] = block
        part = lax.dot_general(
            feats[:, cols], block, (((1,), (1,)), ((), ())), preferred_element_type=jnp.float32
        )
        column = target[step * (span // tile) + t]
        acc[column] = acc[column] + part

    @pl.when(step == pl.num_programs(0) - 1)
    def _():
        send[...] = acc[...].astype(jnp.bfloat16)


def pool(target, live, cells, weights, feats, n_columns, depth):
    nbrs, npts = cells.shape
    half = feats.shape[0]
    tiles = target.shape[0]
    tile = npts // tiles
    group = min(GROUP, tiles)
    span = group * tile
    smem = pl.BlockSpec(memory_space=pltpu.SMEM)
    return pl.pallas_call(
        pool_kernel,
        grid=(tiles // group,),
        in_specs=[
            smem,
            smem,
            pl.BlockSpec((nbrs, span), lambda i: (0, i)),
            pl.BlockSpec((nbrs, span), lambda i: (0, i)),
            pl.BlockSpec((half, span), lambda i: (0, i)),
        ],
        out_specs=[
            pl.BlockSpec((group, depth, tile), lambda i: (i, 0, 0)),
            pl.BlockSpec((n_columns, half, depth), lambda i: (0, 0, 0)),
        ],
        out_shape=[
            jax.ShapeDtypeStruct((tiles, depth, tile), jnp.bfloat16),
            jax.ShapeDtypeStruct((n_columns, half, depth), jnp.bfloat16),
        ],
        scratch_shapes=[pltpu.VMEM((n_columns, half, depth), jnp.float32)],
        compiler_params=pltpu.CompilerParams(vmem_limit_bytes=POOL_VMEM),
        cost_estimate=cost(2 * half * npts * depth, 24 * nbrs * npts * depth // 8),
        name="pool",
    )(target, live, cells, weights, feats)


def spread_kernel(target, columns, blocks, out):
    step = pl.program_id(0)
    group, _, tile = blocks.shape
    for t in range(group):
        column = target[step * group + t]
        part = jnp.dot(columns[column], blocks[t], preferred_element_type=jnp.float32)
        out[:, t * tile : (t + 1) * tile] = part.astype(jnp.bfloat16)


def spread(target, columns, blocks):
    tiles, depth, tile = blocks.shape
    half = columns.shape[1]
    group = min(GROUP, tiles)
    return pl.pallas_call(
        spread_kernel,
        grid=(tiles // group,),
        in_specs=[
            pl.BlockSpec(memory_space=pltpu.SMEM),
            pl.BlockSpec(columns.shape, lambda i: (0, 0, 0)),
            pl.BlockSpec((group, depth, tile), lambda i: (i, 0, 0)),
        ],
        out_specs=pl.BlockSpec((half, group * tile), lambda i: (0, i)),
        out_shape=jax.ShapeDtypeStruct((half, tiles * tile), jnp.bfloat16),
        compiler_params=pltpu.CompilerParams(vmem_limit_bytes=VMEM_LIMIT),
        cost_estimate=cost(2 * half * tiles * tile * depth, 6 * tiles * tile * depth),
        name="spread",
    )(target, columns, blocks)


def unpack_kernel(inner, gathered, out):
    n_dom = gathered.shape[0]
    outer = n_dom // inner
    half = out.shape[2] // 2
    each = gathered.shape[2] // CHUNK
    for k in range(out.shape[0]):
        place = k // each
        source = place % outer * inner + place // outer
        rows = slice(k % each * CHUNK, (k % each + 1) * CHUNK)
        first = gathered[source, 0, rows, :].astype(jnp.float32)
        second = gathered[source, 1, rows, :].astype(jnp.float32)
        for g in range(out.shape[1] // CHUNK):
            lanes = slice(g * half, (g + 1) * half)
            out[k, g * CHUNK : (g + 1) * CHUNK, :] = jnp.concatenate(
                [first[:, lanes], second[:, lanes]], 1
            )


def unpack(gathered, offsets, full, inner):
    vmem = pl.BlockSpec(memory_space=pltpu.VMEM)
    return pl.pallas_call(
        functools.partial(unpack_kernel, inner),
        in_specs=[vmem],
        out_specs=vmem,
        out_shape=jax.ShapeDtypeStruct((offsets, full, full), jnp.float32),
        compiler_params=pltpu.CompilerParams(vmem_limit_bytes=VMEM_LIMIT),
        name="unpack",
    )(gathered)


def later(value, lane):
    return jnp.where(lane == 0, 0.0, pltpu.roll(value, 1, 1))


def earlier(value, lane):
    depth = value.shape[1]
    return jnp.where(lane == depth - 1, 0.0, pltpu.roll(value, depth - 1, 1))


def conv_kernel_body(chan, grid, wf, wb, latent, message, pp, dd, hh):
    half, depth = grid.shape[2], grid.shape[3]
    full = 2 * half
    n_dom = message.shape[0]

    def cot(c, y, x):
        return grid[c, (12 + y, 27 + 2 * y + x, 27 + 2 * y + x, 48 + y)[x]]

    per = message.shape[1] // CHUNK - 4 * half // CHUNK
    first = pl.multiple_of(chan[0] * half, half)
    for s in range(3):
        for y in range(6):
            for x in range(2):
                for c in range(2):
                    rows = slice(y * full + c * half, y * full + (c + 1) * half)
                    pp[2 * s + x, rows, :] = grid[c, (0, 16, 36)[s] + 2 * y + x]
    lane = lax.broadcasted_iota(jnp.int32, (full, depth), 1)
    for x in range(4):
        for y in range(4):
            grown = jnp.zeros((3 * full, depth), jnp.float32)
            for a in range(3):
                grown = grown + jnp.dot(
                    wf[a],
                    pp[x + a, y * full : (y + 3) * full, :],
                    preferred_element_type=jnp.float32,
                )
            h = (
                grown[full : 2 * full]
                + later(grown[:full], lane)
                + earlier(grown[2 * full :], lane)
            )
            sig = jax.nn.sigmoid(h)
            upper = jnp.concatenate([cot(0, y, x), cot(1, y, x)], 0).astype(jnp.float32)
            dd[x, y * full : (y + 1) * full, :] = (upper * sig * (1.0 + h * (1.0 - sig))).astype(
                jnp.bfloat16
            )
            if x in (1, 2) and y in (1, 2):
                hh[...] = h * sig
                mine = pp[x + 1, pl.ds((y + 1) * full + first, half), :].astype(jnp.float32)
                latent[:, x - 1, y - 1, :] = (mine + hh[pl.ds(first, half), :]).astype(jnp.bfloat16)
    lane = lax.broadcasted_iota(jnp.int32, (half, depth), 1)
    for x in range(2):
        for y in range(2):
            grown = jnp.zeros((3 * half, depth), jnp.float32)
            for a in range(3):
                grown = grown + jnp.dot(
                    wb[a],
                    dd[x + a, y * full : (y + 3) * full, :],
                    preferred_element_type=jnp.float32,
                )
            dx = (
                grown[half : 2 * half]
                + earlier(grown[:half], lane)
                + later(grown[2 * half :], lane)
            )
            own = cot(chan[0], y + 1, x + 1).astype(jnp.float32)
            column = (own + dx).astype(jnp.bfloat16)
            for d in range(n_dom):
                message[d, (2 * y + x) * half : (2 * y + x + 1) * half, :] = column
    moved = []
    for x in range(2):
        for y in range(2):
            own = dd[x + 1, pl.ds((y + 1) * full + first, half), :].astype(jnp.float32)
            moved.append(
                jnp.concatenate(
                    [earlier(own, lane), own, later(own, lane), jnp.zeros_like(own)], 0
                ).astype(jnp.bfloat16)
            )
    for a in range(3):
        total = jnp.zeros((3 * full, 4 * half), jnp.float32)
        for x in range(2):
            for y in range(2):
                total = total + lax.dot_general(
                    pp[x + 1 + a, (y + 1) * full : (y + 4) * full, :],
                    moved[2 * x + y],
                    (((1,), (1,)), ((), ())),
                    preferred_element_type=jnp.float32,
                )
        for b in range(3):
            for e in range(3):
                k = 9 * a + 3 * b + e
                pieces = [
                    total[b * full + g * CHUNK : b * full + (g + 1) * CHUNK, e * half : (e + 1) * half]
                    for g in range(full // CHUNK)
                ]
                row = 4 * half + k % per * CHUNK
                message[k // per, row : row + CHUNK, :] = jnp.concatenate(pieces, 1).astype(
                    jnp.bfloat16
                )
    for k in range(27, n_dom * per):
        row = 4 * half + k % per * CHUNK
        message[k // per, row : row + CHUNK, :] = jnp.zeros((CHUNK, depth), jnp.bfloat16)


def conv_layer(chan, grid, wf, wb, n_dom, per):
    half, depth = grid.shape[2], grid.shape[3]
    full = 2 * half
    vmem = pl.BlockSpec(memory_space=pltpu.VMEM)
    return pl.pallas_call(
        conv_kernel_body,
        in_specs=[pl.BlockSpec(memory_space=pltpu.SMEM), vmem, vmem, vmem],
        out_specs=[vmem, vmem],
        out_shape=[
            jax.ShapeDtypeStruct((half, 2, 2, depth), jnp.bfloat16),
            jax.ShapeDtypeStruct((n_dom, 4 * half + per * CHUNK, depth), jnp.bfloat16),
        ],
        scratch_shapes=[
            pltpu.VMEM((6, 6 * full, depth), jnp.bfloat16),
            pltpu.VMEM((4, 4 * full, depth), jnp.bfloat16),
            pltpu.VMEM((full, depth), jnp.float32),
        ],
        compiler_params=pltpu.CompilerParams(vmem_limit_bytes=VMEM_LIMIT),
        name="conv_layer",
    )(chan, grid, wf, wb)


def neighbours(first, last, axis):
    peers = lax.axis_size(axis)
    up = [(i, i + 1) for i in range(peers - 1)]
    down = [(j, i) for i, j in up]
    return lax.ppermute(last, axis, up), lax.ppermute(first, axis, down)


def body(
    point_features,
    neighbour_cells,
    neighbour_weights,
    live_points,
    tile_target,
    conv_kernel,
    cotangent,
):
    half = point_features.shape[0]
    full = 2 * half
    xsize, ysize, depth = cotangent.shape[1:]
    n_dom, n_slab = lax.axis_size("dom"), lax.axis_size("slab")
    width = xsize * ysize
    chan = lax.axis_index("chan").astype(jnp.int32)
    scale = float(width * depth * n_dom * n_slab) ** (-0.5)

    blocks, send = pool(
        tile_target,
        live_points,
        neighbour_cells,
        neighbour_weights,
        point_features,
        n_dom * width,
        depth,
    )

    kernel = conv_kernel.reshape(3, 3, 3, full, full)
    wf = kernel.transpose(0, 2, 4, 1, 3).reshape(3, 3 * full, 3 * full)
    wb = lax.dynamic_slice_in_dim(kernel[::-1, ::-1], chan * half, half, 3)
    wb = wb.transpose(0, 2, 3, 1, 4).reshape(3, 3 * half, 3 * full)

    inner = min(8, n_dom // 2)
    outer = n_dom // inner
    same_z = [[x * inner + z for x in range(outer)] for z in range(inner)]
    same_x = [[x * inner + z for z in range(inner)] for x in range(outer)]

    def exchange(value, axis, groups=None):
        return lax.all_to_all(
            value, axis, split_axis=0, concat_axis=0, tiled=True, axis_index_groups=groups
        )

    def total(value, parts):
        return value.reshape((parts, -1) + value.shape[1:]).astype(jnp.float32).sum(0)

    part = total(exchange(send, "dom", same_z), outer).astype(jnp.bfloat16)
    part = exchange(part, "dom", same_x)
    part, wf, wb = lax.optimization_barrier((part, wf, wb))
    pooled = total(part, inner).astype(jnp.bfloat16)

    cot = cotangent.transpose(2, 1, 0, 3)
    before, after = neighbours(
        jnp.concatenate([pooled, cot[0]], 0), jnp.concatenate([pooled, cot[-1]], 0), "dom"
    )
    pooled = jnp.concatenate([before[:width], pooled, after[:width]], 0)
    cot = jnp.concatenate([before[None, width:], cot, after[None, width:]], 0)
    before, after = neighbours(
        jnp.concatenate([pooled, cot[:, 0]], 0), jnp.concatenate([pooled, cot[:, -1]], 0), "slab"
    )
    grid = jnp.concatenate([before, pooled, cot.reshape((-1,) + cot.shape[2:]), after], 0)
    grid = lax.all_gather(grid, "chan", axis=0, tiled=False)

    each = -(-27 // n_dom)
    latent, message = conv_layer(chan[None], grid, wf, wb, inner, outer * each)
    message = exchange(message, "dom", same_x)
    columns = message[:, : width * half].reshape(inner * width, half, depth)
    columns = lax.all_gather(columns, "dom", axis=0, tiled=True, axis_index_groups=same_z)

    peers = 2 * n_slab
    same_z_all = [
        [(x * inner + z) * peers + p for x in range(outer) for p in range(peers)]
        for z in range(inner)
    ]
    kgrad = message[:, width * half :].astype(jnp.float32).sum(0).astype(jnp.bfloat16)
    kgrad = kgrad.reshape(outer, 1, each * CHUNK, depth)
    kgrad = jnp.broadcast_to(kgrad, (outer, peers, each * CHUNK, depth))
    kgrad = exchange(
        kgrad.reshape(outer * peers, each * CHUNK, depth), ("dom", "slab", "chan"), same_z_all
    )
    kgrad = (total(kgrad, outer * n_slab) * scale).astype(jnp.bfloat16)
    kgrad = exchange(jnp.broadcast_to(kgrad[None], (n_dom,) + kgrad.shape), "dom")
    feature_grad = spread(tile_target, columns, blocks)
    kgrad, feature_grad = lax.optimization_barrier((kgrad, feature_grad))
    kernel_grad = unpack(kgrad, 27, full, inner)
    return (latent, feature_grad, kernel_grad)


def solution(mesh):
    placed = (
        P("chan", ("dom", "slab")),
        P(None, ("dom", "slab")),
        P(None, ("dom", "slab")),
        P(("dom", "slab")),
        P(("dom", "slab")),
        P(),
        P("chan", "slab", "dom", None),
    )
    return jax.shard_map(
        body,
        mesh=mesh,
        in_specs=placed,
        out_specs=(P("chan", "slab", "dom", None), P("chan", ("dom", "slab")), P()),
        check_vma=False,
    )
```

```python
import functools

import jax
import jax.numpy as jnp
from jax import lax
from jax.experimental import pallas as pl
from jax.experimental.pallas import tpu as pltpu
from jax.sharding import PartitionSpec as P

POOL_GROUP = 32
SPREAD_GROUP = 16
POOL_VMEM = 60 * 1024 * 1024
VMEM_LIMIT = 16 * 1024 * 1024
CHUNK = 16


def cost(flops, moved):
    return pl.CostEstimate(flops=flops, bytes_accessed=moved, transcendentals=0)


def pool_kernel(target, live, cells, weights, feats, blocks, send, acc):
    step = pl.program_id(0)
    tile = blocks.shape[2]
    depth = blocks.shape[1]

    @pl.when(step == 0)
    def _():
        acc[...] = jnp.zeros_like(acc)

    span = cells.shape[1]
    position = step * span + lax.broadcasted_iota(jnp.int32, cells.shape, 1)
    masked = jnp.where(position < live[0], weights[...], 0.0)
    cell = cells[...].astype(jnp.float32)
    depth_ids = lax.broadcasted_iota(jnp.int32, (depth, tile), 0)
    depth_ids = depth_ids.astype(jnp.float32).astype(jnp.bfloat16)

    def spread_rows(row):
        return jnp.broadcast_to(row, (depth, tile)).astype(jnp.bfloat16)

    for t in range(span // tile):
        cols = slice(t * tile, (t + 1) * tile)
        terms = []
        for k in range(cells.shape[0]):
            weight = spread_rows(masked[k : k + 1, cols])
            here = spread_rows(cell[k : k + 1, cols]) == depth_ids
            terms.append(jnp.where(here, weight, jnp.zeros_like(weight)))
        while len(terms) > 1:
            terms = [one + two for one, two in zip(terms[::2], terms[1::2])]
        block = terms[0]
        blocks[t] = block
        part = lax.dot_general(
            feats[:, cols], block, (((1,), (1,)), ((), ())), preferred_element_type=jnp.float32
        )
        column = target[step * (span // tile) + t]
        acc[column] = acc[column] + part

    @pl.when(step == pl.num_programs(0) - 1)
    def _():
        send[...] = acc[...].astype(jnp.bfloat16)


def pool(target, live, cells, weights, feats, n_columns, depth):
    nbrs, npts = cells.shape
    half = feats.shape[0]
    tiles = target.shape[0]
    tile = npts // tiles
    group = min(POOL_GROUP, tiles)
    span = group * tile
    smem = pl.BlockSpec(memory_space=pltpu.SMEM)
    return pl.pallas_call(
        pool_kernel,
        grid=(tiles // group,),
        in_specs=[
            smem,
            smem,
            pl.BlockSpec((nbrs, span), lambda i: (0, i)),
            pl.BlockSpec((nbrs, span), lambda i: (0, i)),
            pl.BlockSpec((half, span), lambda i: (0, i)),
        ],
        out_specs=[
            pl.BlockSpec((group, depth, tile), lambda i: (i, 0, 0)),
            pl.BlockSpec((n_columns, half, depth), lambda i: (0, 0, 0)),
        ],
        out_shape=[
            jax.ShapeDtypeStruct((tiles, depth, tile), jnp.bfloat16),
            jax.ShapeDtypeStruct((n_columns, half, depth), jnp.bfloat16),
        ],
        scratch_shapes=[pltpu.VMEM((n_columns, half, depth), jnp.float32)],
        compiler_params=pltpu.CompilerParams(vmem_limit_bytes=POOL_VMEM),
        cost_estimate=cost(2 * half * npts * depth, 24 * nbrs * npts * depth // 8),
        name="pool",
    )(target, live, cells, weights, feats)


def spread_kernel(target, place, *refs):
    *parts, blocks, out, columns = refs
    step = pl.program_id(0)
    group, _, tile = blocks.shape
    count = parts[0].shape[0]

    @pl.when(step == 0)
    def _():
        for shift, part in enumerate(parts):
            source = lax.rem(place[0] + (len(parts) - shift), len(parts))
            columns[pl.ds(source * count, count)] = part[...]

    for t in range(group):
        column = target[step * group + t]
        value = jnp.dot(columns[column], blocks[t], preferred_element_type=jnp.float32)
        out[:, t * tile : (t + 1) * tile] = value.astype(jnp.bfloat16)


def spread(target, place, parts, blocks):
    tiles, depth, tile = blocks.shape
    count, half, _ = parts[0].shape
    group = min(SPREAD_GROUP, tiles)
    smem = pl.BlockSpec(memory_space=pltpu.SMEM)
    return pl.pallas_call(
        spread_kernel,
        grid=(tiles // group,),
        in_specs=[smem, smem]
        + [pl.BlockSpec(part.shape, lambda i: (0, 0, 0)) for part in parts]
        + [pl.BlockSpec((group, depth, tile), lambda i: (i, 0, 0))],
        out_specs=pl.BlockSpec((half, group * tile), lambda i: (0, i)),
        out_shape=jax.ShapeDtypeStruct((half, tiles * tile), jnp.bfloat16),
        scratch_shapes=[pltpu.VMEM((count * len(parts), half, depth), jnp.bfloat16)],
        compiler_params=pltpu.CompilerParams(vmem_limit_bytes=VMEM_LIMIT),
        cost_estimate=cost(2 * half * tiles * tile * depth, 6 * tiles * tile * depth),
        name="spread",
    )(target, place, *parts, blocks)


def unpack_kernel(inner, gathered, out):
    n_dom = gathered.shape[0]
    outer = n_dom // inner
    half = out.shape[2] // 2
    each = gathered.shape[2] // CHUNK
    for k in range(out.shape[0]):
        place = k // each
        source = place % outer * inner + place // outer
        rows = slice(k % each * CHUNK, (k % each + 1) * CHUNK)
        first = gathered[source, 0, rows, :].astype(jnp.float32)
        second = gathered[source, 1, rows, :].astype(jnp.float32)
        for g in range(out.shape[1] // CHUNK):
            lanes = slice(g * half, (g + 1) * half)
            out[k, g * CHUNK : (g + 1) * CHUNK, :] = jnp.concatenate(
                [first[:, lanes], second[:, lanes]], 1
            )


def unpack(gathered, offsets, full, inner):
    vmem = pl.BlockSpec(memory_space=pltpu.VMEM)
    return pl.pallas_call(
        functools.partial(unpack_kernel, inner),
        in_specs=[vmem],
        out_specs=vmem,
        out_shape=jax.ShapeDtypeStruct((offsets, full, full), jnp.float32),
        compiler_params=pltpu.CompilerParams(vmem_limit_bytes=VMEM_LIMIT),
        name="unpack",
    )(gathered)


def later(value, lane):
    return jnp.where(lane == 0, 0.0, pltpu.roll(value, 1, 1))


def earlier(value, lane):
    depth = value.shape[1]
    return jnp.where(lane == depth - 1, 0.0, pltpu.roll(value, depth - 1, 1))


def conv_kernel_body(chan, grid, wf, wb, latent, message, pp, dd, hh):
    half, depth = grid.shape[2], grid.shape[3]
    full = 2 * half
    n_dom = message.shape[0]

    def cot(c, y, x):
        return grid[c, (12 + y, 27 + 2 * y + x, 27 + 2 * y + x, 48 + y)[x]]

    per = message.shape[1] // CHUNK - 4 * half // CHUNK
    first = pl.multiple_of(chan[0] * half, half)
    for s in range(3):
        for y in range(6):
            for x in range(2):
                for c in range(2):
                    rows = slice(y * full + c * half, y * full + (c + 1) * half)
                    pp[2 * s + x, rows, :] = grid[c, (0, 16, 36)[s] + 2 * y + x]
    lane = lax.broadcasted_iota(jnp.int32, (full, depth), 1)
    for x in range(4):
        for y in range(4):
            grown = jnp.zeros((3 * full, depth), jnp.float32)
            for a in range(3):
                grown = grown + jnp.dot(
                    wf[a],
                    pp[x + a, y * full : (y + 3) * full, :],
                    preferred_element_type=jnp.float32,
                )
            h = (
                grown[full : 2 * full]
                + later(grown[:full], lane)
                + earlier(grown[2 * full :], lane)
            )
            sig = jax.nn.sigmoid(h)
            upper = jnp.concatenate([cot(0, y, x), cot(1, y, x)], 0).astype(jnp.float32)
            dd[x, y * full : (y + 1) * full, :] = (upper * sig * (1.0 + h * (1.0 - sig))).astype(
                jnp.bfloat16
            )
            if x in (1, 2) and y in (1, 2):
                hh[...] = h * sig
                mine = pp[x + 1, pl.ds((y + 1) * full + first, half), :].astype(jnp.float32)
                latent[:, x - 1, y - 1, :] = (mine + hh[pl.ds(first, half), :]).astype(jnp.bfloat16)
    lane = lax.broadcasted_iota(jnp.int32, (half, depth), 1)
    for x in range(2):
        for y in range(2):
            grown = jnp.zeros((3 * half, depth), jnp.float32)
            for a in range(3):
                grown = grown + jnp.dot(
                    wb[a],
                    dd[x + a, y * full : (y + 3) * full, :],
                    preferred_element_type=jnp.float32,
                )
            dx = (
                grown[half : 2 * half]
                + earlier(grown[:half], lane)
                + later(grown[2 * half :], lane)
            )
            own = cot(chan[0], y + 1, x + 1).astype(jnp.float32)
            column = (own + dx).astype(jnp.bfloat16)
            for d in range(n_dom):
                message[d, (2 * y + x) * half : (2 * y + x + 1) * half, :] = column
    moved = []
    for x in range(2):
        for y in range(2):
            own = dd[x + 1, pl.ds((y + 1) * full + first, half), :].astype(jnp.float32)
            moved.append(
                jnp.concatenate(
                    [earlier(own, lane), own, later(own, lane), jnp.zeros_like(own)], 0
                ).astype(jnp.bfloat16)
            )
    for a in range(3):
        total = jnp.zeros((3 * full, 4 * half), jnp.float32)
        for x in range(2):
            for y in range(2):
                total = total + lax.dot_general(
                    pp[x + 1 + a, (y + 1) * full : (y + 4) * full, :],
                    moved[2 * x + y],
                    (((1,), (1,)), ((), ())),
                    preferred_element_type=jnp.float32,
                )
        for b in range(3):
            for e in range(3):
                k = 9 * a + 3 * b + e
                pieces = [
                    total[b * full + g * CHUNK : b * full + (g + 1) * CHUNK, e * half : (e + 1) * half]
                    for g in range(full // CHUNK)
                ]
                row = 4 * half + k % per * CHUNK
                message[k // per, row : row + CHUNK, :] = jnp.concatenate(pieces, 1).astype(
                    jnp.bfloat16
                )
    for k in range(27, n_dom * per):
        row = 4 * half + k % per * CHUNK
        message[k // per, row : row + CHUNK, :] = jnp.zeros((CHUNK, depth), jnp.bfloat16)


def conv_layer(chan, grid, wf, wb, n_dom, per):
    half, depth = grid.shape[2], grid.shape[3]
    full = 2 * half
    vmem = pl.BlockSpec(memory_space=pltpu.VMEM)
    return pl.pallas_call(
        conv_kernel_body,
        in_specs=[pl.BlockSpec(memory_space=pltpu.SMEM), vmem, vmem, vmem],
        out_specs=[vmem, vmem],
        out_shape=[
            jax.ShapeDtypeStruct((half, 2, 2, depth), jnp.bfloat16),
            jax.ShapeDtypeStruct((n_dom, 4 * half + per * CHUNK, depth), jnp.bfloat16),
        ],
        scratch_shapes=[
            pltpu.VMEM((6, 6 * full, depth), jnp.bfloat16),
            pltpu.VMEM((4, 4 * full, depth), jnp.bfloat16),
            pltpu.VMEM((full, depth), jnp.float32),
        ],
        compiler_params=pltpu.CompilerParams(vmem_limit_bytes=VMEM_LIMIT),
        name="conv_layer",
    )(chan, grid, wf, wb)


def neighbours(first, last, axis):
    peers = lax.axis_size(axis)
    up = [(i, i + 1) for i in range(peers - 1)]
    down = [(j, i) for i, j in up]
    return lax.ppermute(last, axis, up), lax.ppermute(first, axis, down)


def body(
    point_features,
    neighbour_cells,
    neighbour_weights,
    live_points,
    tile_target,
    conv_kernel,
    cotangent,
):
    half = point_features.shape[0]
    full = 2 * half
    xsize, ysize, depth = cotangent.shape[1:]
    n_dom, n_slab = lax.axis_size("dom"), lax.axis_size("slab")
    width = xsize * ysize
    chan = lax.axis_index("chan").astype(jnp.int32)
    place = (lax.axis_index("dom") // min(8, n_dom // 2)).astype(jnp.int32)
    scale = float(width * depth * n_dom * n_slab) ** (-0.5)

    blocks, send = pool(
        tile_target,
        live_points,
        neighbour_cells,
        neighbour_weights,
        point_features,
        n_dom * width,
        depth,
    )

    kernel = conv_kernel.reshape(3, 3, 3, full, full)
    wf = kernel.transpose(0, 2, 4, 1, 3).reshape(3, 3 * full, 3 * full)
    wb = lax.dynamic_slice_in_dim(kernel[::-1, ::-1], chan * half, half, 3)
    wb = wb.transpose(0, 2, 3, 1, 4).reshape(3, 3 * half, 3 * full)

    inner = min(8, n_dom // 2)
    outer = n_dom // inner
    same_z = [[x * inner + z for x in range(outer)] for z in range(inner)]
    same_x = [[x * inner + z for z in range(inner)] for x in range(outer)]

    def exchange(value, axis, groups=None):
        return lax.all_to_all(
            value, axis, split_axis=0, concat_axis=0, tiled=True, axis_index_groups=groups
        )

    def total(value, parts):
        return value.reshape((parts, -1) + value.shape[1:]).astype(jnp.float32).sum(0)

    part = total(exchange(send, "dom", same_z), outer).astype(jnp.bfloat16)
    part = exchange(part, "dom", same_x)
    part, wf, wb = lax.optimization_barrier((part, wf, wb))
    pooled = total(part, inner).astype(jnp.bfloat16)

    cot = cotangent.transpose(2, 1, 0, 3)
    before, after = neighbours(
        jnp.concatenate([pooled, cot[0]], 0), jnp.concatenate([pooled, cot[-1]], 0), "dom"
    )
    pooled = jnp.concatenate([before[:width], pooled, after[:width]], 0)
    cot = jnp.concatenate([before[None, width:], cot, after[None, width:]], 0)
    before, after = neighbours(
        jnp.concatenate([pooled, cot[:, 0]], 0), jnp.concatenate([pooled, cot[:, -1]], 0), "slab"
    )
    grid = jnp.concatenate([before, pooled, cot.reshape((-1,) + cot.shape[2:]), after], 0)
    grid = lax.all_gather(grid, "chan", axis=0, tiled=False)

    each = -(-27 // n_dom)
    latent, message = conv_layer(chan[None], grid, wf, wb, inner, outer * each)
    message = exchange(message, "dom", same_x)
    columns = message[:, : width * half].reshape(inner * width, half, depth)
    columns = [columns] + [
        lax.ppermute(
            columns, "dom", [(g[x], g[(x + shift) % outer]) for g in same_z for x in range(outer)]
        )
        for shift in range(1, outer)
    ]

    peers = 2 * n_slab
    same_z_all = [
        [(x * inner + z) * peers + p for x in range(outer) for p in range(peers)]
        for z in range(inner)
    ]
    kgrad = message[:, width * half :].astype(jnp.float32).sum(0).astype(jnp.bfloat16)
    kgrad = kgrad.reshape(outer, 1, each * CHUNK, depth)
    kgrad = jnp.broadcast_to(kgrad, (outer, peers, each * CHUNK, depth))
    kgrad = exchange(
        kgrad.reshape(outer * peers, each * CHUNK, depth), ("dom", "slab", "chan"), same_z_all
    )
    kgrad = (total(kgrad, outer * n_slab) * scale).astype(jnp.bfloat16)
    kgrad, columns = lax.optimization_barrier((kgrad, columns))
    kgrad = exchange(jnp.broadcast_to(kgrad[None], (n_dom,) + kgrad.shape), "dom")
    feature_grad = spread(tile_target, place[None], columns, blocks)
    kgrad, feature_grad = lax.optimization_barrier((kgrad, feature_grad))
    kernel_grad = unpack(kgrad, 27, full, inner)
    return (latent, feature_grad, kernel_grad)


def solution(mesh):
    placed = (
        P("chan", ("dom", "slab")),
        P(None, ("dom", "slab")),
        P(None, ("dom", "slab")),
        P(("dom", "slab")),
        P(("dom", "slab")),
        P(),
        P("chan", "slab", "dom", None),
    )
    return jax.shard_map(
        body,
        mesh=mesh,
        in_specs=placed,
        out_specs=(P("chan", "slab", "dom", None), P("chan", ("dom", "slab")), P()),
        check_vma=False,
    )
```

```python
import functools

import jax
import jax.numpy as jnp
from jax import lax
from jax.experimental import pallas as pl
from jax.experimental.pallas import tpu as pltpu
from jax.sharding import PartitionSpec as P

POOL_GROUP = 32
SPREAD_GROUP = 16
POOL_VMEM = 60 * 1024 * 1024
VMEM_LIMIT = 16 * 1024 * 1024
CHUNK = 16


def cost(flops, moved):
    return pl.CostEstimate(flops=flops, bytes_accessed=moved, transcendentals=0)


def pool_kernel(target, live, cells, weights, feats, blocks, send, acc):
    step = pl.program_id(0)
    tile = blocks.shape[2]
    depth = blocks.shape[1]

    @pl.when(step == 0)
    def _():
        acc[...] = jnp.zeros_like(acc)

    span = cells.shape[1]
    position = step * span + lax.broadcasted_iota(jnp.int32, cells.shape, 1)
    masked = jnp.where(position < live[0], weights[...], 0.0)
    cell = cells[...].astype(jnp.float32)
    depth_ids = lax.broadcasted_iota(jnp.int32, (depth, tile), 0)
    depth_ids = depth_ids.astype(jnp.float32).astype(jnp.bfloat16)

    def spread_rows(row):
        return jnp.broadcast_to(row, (depth, tile)).astype(jnp.bfloat16)

    for t in range(span // tile):
        cols = slice(t * tile, (t + 1) * tile)
        terms = []
        for k in range(cells.shape[0]):
            weight = spread_rows(masked[k : k + 1, cols])
            here = spread_rows(cell[k : k + 1, cols]) == depth_ids
            terms.append(jnp.where(here, weight, jnp.zeros_like(weight)))
        while len(terms) > 1:
            terms = [one + two for one, two in zip(terms[::2], terms[1::2])]
        block = terms[0]
        blocks[t] = block
        part = lax.dot_general(
            feats[:, cols], block, (((1,), (1,)), ((), ())), preferred_element_type=jnp.float32
        )
        column = target[step * (span // tile) + t]
        acc[column] = acc[column] + part

    @pl.when(step == pl.num_programs(0) - 1)
    def _():
        send[...] = acc[...].astype(jnp.bfloat16)


def pool(target, live, cells, weights, feats, n_columns, depth):
    nbrs, npts = cells.shape
    half = feats.shape[0]
    tiles = target.shape[0]
    tile = npts // tiles
    group = min(POOL_GROUP, tiles)
    span = group * tile
    smem = pl.BlockSpec(memory_space=pltpu.SMEM)
    return pl.pallas_call(
        pool_kernel,
        grid=(tiles // group,),
        in_specs=[
            smem,
            smem,
            pl.BlockSpec((nbrs, span), lambda i: (0, i)),
            pl.BlockSpec((nbrs, span), lambda i: (0, i)),
            pl.BlockSpec((half, span), lambda i: (0, i)),
        ],
        out_specs=[
            pl.BlockSpec((group, depth, tile), lambda i: (i, 0, 0)),
            pl.BlockSpec((n_columns, half, depth), lambda i: (0, 0, 0)),
        ],
        out_shape=[
            jax.ShapeDtypeStruct((tiles, depth, tile), jnp.bfloat16),
            jax.ShapeDtypeStruct((n_columns, half, depth), jnp.bfloat16),
        ],
        scratch_shapes=[pltpu.VMEM((n_columns, half, depth), jnp.float32)],
        compiler_params=pltpu.CompilerParams(vmem_limit_bytes=POOL_VMEM),
        cost_estimate=cost(2 * half * npts * depth, 24 * nbrs * npts * depth // 8),
        name="pool",
    )(target, live, cells, weights, feats)


def spread_kernel(inner, target, columns, blocks, out):
    step = pl.program_id(0)
    group, _, tile = blocks.shape
    half = out.shape[0]
    for t in range(group):
        column = target[step * group + t]
        first = pl.multiple_of(column % inner * half, half)
        own = columns[column // inner, pl.ds(first, half), :]
        value = jnp.dot(own, blocks[t], preferred_element_type=jnp.float32)
        out[:, t * tile : (t + 1) * tile] = value.astype(jnp.bfloat16)


def spread(target, columns, blocks, half, inner):
    tiles, depth, tile = blocks.shape
    group = min(SPREAD_GROUP, tiles)
    return pl.pallas_call(
        functools.partial(spread_kernel, inner),
        grid=(tiles // group,),
        in_specs=[
            pl.BlockSpec(memory_space=pltpu.SMEM),
            pl.BlockSpec(columns.shape, lambda i: (0, 0, 0)),
            pl.BlockSpec((group, depth, tile), lambda i: (i, 0, 0)),
        ],
        out_specs=pl.BlockSpec((half, group * tile), lambda i: (0, i)),
        out_shape=jax.ShapeDtypeStruct((half, tiles * tile), jnp.bfloat16),
        compiler_params=pltpu.CompilerParams(vmem_limit_bytes=VMEM_LIMIT),
        cost_estimate=cost(2 * half * tiles * tile * depth, 6 * tiles * tile * depth),
        name="spread",
    )(target, columns, blocks)


def in_vmem(kernel, name, out_shape, *args):
    vmem = pl.BlockSpec(memory_space=pltpu.VMEM)
    return pl.pallas_call(
        kernel,
        in_specs=[vmem] * len(args),
        out_specs=vmem,
        out_shape=jax.ShapeDtypeStruct(out_shape, jnp.bfloat16),
        compiler_params=pltpu.CompilerParams(vmem_limit_bytes=VMEM_LIMIT),
        name=name,
    )(*args)


def added(parts):
    total = parts[0].astype(jnp.float32)
    for part in parts[1:]:
        total = total + part.astype(jnp.float32)
    return total


def add_kernel(received, out):
    count = out.shape[0]
    for d in range(count):
        parts = [received[first + d] for first in range(0, received.shape[0], count)]
        out[d] = added(parts).astype(jnp.bfloat16)


def relay_kernel(own, received, message):
    sources = received.shape[0]
    outer = message.shape[0]
    total = added([received[z, own:, :] for z in range(sources)]).astype(jnp.bfloat16)
    rows = total.shape[0] // outer
    for x in range(outer):
        for z in range(sources):
            message[x, z * own : (z + 1) * own, :] = received[z, :own, :]
        message[x, sources * own :, :] = total[x * rows : (x + 1) * rows]


def share_kernel(received, message):
    first = received.shape[1] - message.shape[1]
    total = added([received[x, first:, :] for x in range(received.shape[0])])
    total = total.astype(jnp.bfloat16)
    for peer in range(message.shape[0]):
        message[peer] = total


def finish_kernel(scale, received, message):
    for c in range(2):
        total = added([received[s + c] for s in range(0, received.shape[0], 2)]) * scale
        total = total.astype(jnp.bfloat16)
        for peer in range(message.shape[0]):
            message[peer, c] = total


def unpack_kernel(inner, gathered, out):
    n_dom = gathered.shape[0]
    outer = n_dom // inner
    half = out.shape[2] // 2
    each = gathered.shape[2] // CHUNK
    for k in range(out.shape[0]):
        place = k // each
        source = place % outer * inner + place // outer
        rows = slice(k % each * CHUNK, (k % each + 1) * CHUNK)
        first = gathered[source, 0, rows, :].astype(jnp.float32)
        second = gathered[source, 1, rows, :].astype(jnp.float32)
        for g in range(out.shape[1] // CHUNK):
            lanes = slice(g * half, (g + 1) * half)
            out[k, g * CHUNK : (g + 1) * CHUNK, :] = jnp.concatenate(
                [first[:, lanes], second[:, lanes]], 1
            )


def unpack(gathered, offsets, full, inner):
    vmem = pl.BlockSpec(memory_space=pltpu.VMEM)
    return pl.pallas_call(
        functools.partial(unpack_kernel, inner),
        in_specs=[vmem],
        out_specs=vmem,
        out_shape=jax.ShapeDtypeStruct((offsets, full, full), jnp.float32),
        compiler_params=pltpu.CompilerParams(vmem_limit_bytes=VMEM_LIMIT),
        name="unpack",
    )(gathered)


def later(value, lane):
    return jnp.where(lane == 0, 0.0, pltpu.roll(value, 1, 1))


def earlier(value, lane):
    depth = value.shape[1]
    return jnp.where(lane == depth - 1, 0.0, pltpu.roll(value, depth - 1, 1))


def conv_kernel_body(chan, grid, wf, wb, latent, message, pp, dd, hh):
    half, depth = grid.shape[2], grid.shape[3]
    full = 2 * half
    n_dom = message.shape[0]

    def cot(c, y, x):
        return grid[c, (12 + y, 27 + 2 * y + x, 27 + 2 * y + x, 48 + y)[x]]

    per = message.shape[1] // CHUNK - 4 * half // CHUNK
    first = pl.multiple_of(chan[0] * half, half)
    for s in range(3):
        for y in range(6):
            for x in range(2):
                for c in range(2):
                    rows = slice(y * full + c * half, y * full + (c + 1) * half)
                    pp[2 * s + x, rows, :] = grid[c, (0, 16, 36)[s] + 2 * y + x]
    lane = lax.broadcasted_iota(jnp.int32, (full, depth), 1)
    for x in range(4):
        for y in range(4):
            grown = jnp.zeros((3 * full, depth), jnp.float32)
            for a in range(3):
                grown = grown + jnp.dot(
                    wf[a],
                    pp[x + a, y * full : (y + 3) * full, :],
                    preferred_element_type=jnp.float32,
                )
            h = (
                grown[full : 2 * full]
                + later(grown[:full], lane)
                + earlier(grown[2 * full :], lane)
            )
            sig = jax.nn.sigmoid(h)
            upper = jnp.concatenate([cot(0, y, x), cot(1, y, x)], 0).astype(jnp.float32)
            dd[x, y * full : (y + 1) * full, :] = (upper * sig * (1.0 + h * (1.0 - sig))).astype(
                jnp.bfloat16
            )
            if x in (1, 2) and y in (1, 2):
                hh[...] = h * sig
                mine = pp[x + 1, pl.ds((y + 1) * full + first, half), :].astype(jnp.float32)
                latent[:, x - 1, y - 1, :] = (mine + hh[pl.ds(first, half), :]).astype(jnp.bfloat16)
    lane = lax.broadcasted_iota(jnp.int32, (half, depth), 1)
    for x in range(2):
        for y in range(2):
            grown = jnp.zeros((3 * half, depth), jnp.float32)
            for a in range(3):
                grown = grown + jnp.dot(
                    wb[a],
                    dd[x + a, y * full : (y + 3) * full, :],
                    preferred_element_type=jnp.float32,
                )
            dx = (
                grown[half : 2 * half]
                + earlier(grown[:half], lane)
                + later(grown[2 * half :], lane)
            )
            own = cot(chan[0], y + 1, x + 1).astype(jnp.float32)
            column = (own + dx).astype(jnp.bfloat16)
            for d in range(n_dom):
                message[d, (2 * y + x) * half : (2 * y + x + 1) * half, :] = column
    moved = []
    for x in range(2):
        for y in range(2):
            own = dd[x + 1, pl.ds((y + 1) * full + first, half), :].astype(jnp.float32)
            moved.append(
                jnp.concatenate(
                    [earlier(own, lane), own, later(own, lane), jnp.zeros_like(own)], 0
                ).astype(jnp.bfloat16)
            )
    for a in range(3):
        total = jnp.zeros((3 * full, 4 * half), jnp.float32)
        for x in range(2):
            for y in range(2):
                total = total + lax.dot_general(
                    pp[x + 1 + a, (y + 1) * full : (y + 4) * full, :],
                    moved[2 * x + y],
                    (((1,), (1,)), ((), ())),
                    preferred_element_type=jnp.float32,
                )
        for b in range(3):
            for e in range(3):
                k = 9 * a + 3 * b + e
                pieces = [
                    total[b * full + g * CHUNK : b * full + (g + 1) * CHUNK, e * half : (e + 1) * half]
                    for g in range(full // CHUNK)
                ]
                row = 4 * half + k % per * CHUNK
                message[k // per, row : row + CHUNK, :] = jnp.concatenate(pieces, 1).astype(
                    jnp.bfloat16
                )
    for k in range(27, n_dom * per):
        row = 4 * half + k % per * CHUNK
        message[k // per, row : row + CHUNK, :] = jnp.zeros((CHUNK, depth), jnp.bfloat16)


def conv_layer(chan, grid, wf, wb, n_dom, per):
    half, depth = grid.shape[2], grid.shape[3]
    full = 2 * half
    vmem = pl.BlockSpec(memory_space=pltpu.VMEM)
    return pl.pallas_call(
        conv_kernel_body,
        in_specs=[pl.BlockSpec(memory_space=pltpu.SMEM), vmem, vmem, vmem],
        out_specs=[vmem, vmem],
        out_shape=[
            jax.ShapeDtypeStruct((half, 2, 2, depth), jnp.bfloat16),
            jax.ShapeDtypeStruct((n_dom, 4 * half + per * CHUNK, depth), jnp.bfloat16),
        ],
        scratch_shapes=[
            pltpu.VMEM((6, 6 * full, depth), jnp.bfloat16),
            pltpu.VMEM((4, 4 * full, depth), jnp.bfloat16),
            pltpu.VMEM((full, depth), jnp.float32),
        ],
        compiler_params=pltpu.CompilerParams(vmem_limit_bytes=VMEM_LIMIT),
        name="conv_layer",
    )(chan, grid, wf, wb)


def neighbours(first, last, axis):
    peers = lax.axis_size(axis)
    up = [(i, i + 1) for i in range(peers - 1)]
    down = [(j, i) for i, j in up]
    return lax.ppermute(last, axis, up), lax.ppermute(first, axis, down)


def body(
    point_features,
    neighbour_cells,
    neighbour_weights,
    live_points,
    tile_target,
    conv_kernel,
    cotangent,
):
    half = point_features.shape[0]
    full = 2 * half
    xsize, ysize, depth = cotangent.shape[1:]
    n_dom, n_slab = lax.axis_size("dom"), lax.axis_size("slab")
    width = xsize * ysize
    chan = lax.axis_index("chan").astype(jnp.int32)
    scale = float(width * depth * n_dom * n_slab) ** (-0.5)

    blocks, send = pool(
        tile_target,
        live_points,
        neighbour_cells,
        neighbour_weights,
        point_features,
        n_dom * width,
        depth,
    )

    kernel = conv_kernel.reshape(3, 3, 3, full, full)
    wf = kernel.transpose(0, 2, 4, 1, 3).reshape(3, 3 * full, 3 * full)
    wb = lax.dynamic_slice_in_dim(kernel[::-1, ::-1], chan * half, half, 3)
    wb = wb.transpose(0, 2, 3, 1, 4).reshape(3, 3 * half, 3 * full)

    inner = min(8, n_dom // 2)
    outer = n_dom // inner
    same_z = [[x * inner + z for x in range(outer)] for z in range(inner)]
    same_x = [[x * inner + z for z in range(inner)] for x in range(outer)]

    def exchange(value, axis, groups=None):
        return lax.all_to_all(
            value, axis, split_axis=0, concat_axis=0, tiled=True, axis_index_groups=groups
        )

    def total(value, parts):
        return value.reshape((parts, -1) + value.shape[1:]).astype(jnp.float32).sum(0)

    part = exchange(send, "dom", same_z)
    part = in_vmem(add_kernel, "add_x", (part.shape[0] // outer,) + part.shape[1:], part)
    part = exchange(part, "dom", same_x)
    part, wf, wb = lax.optimization_barrier((part, wf, wb))
    pooled = total(part, inner).astype(jnp.bfloat16)

    cot = cotangent.transpose(2, 1, 0, 3)
    before, after = neighbours(
        jnp.concatenate([pooled, cot[0]], 0), jnp.concatenate([pooled, cot[-1]], 0), "dom"
    )
    pooled = jnp.concatenate([before[:width], pooled, after[:width]], 0)
    cot = jnp.concatenate([before[None, width:], cot, after[None, width:]], 0)
    before, after = neighbours(
        jnp.concatenate([pooled, cot[:, 0]], 0), jnp.concatenate([pooled, cot[:, -1]], 0), "slab"
    )
    grid = jnp.concatenate([before, pooled, cot.reshape((-1,) + cot.shape[2:]), after], 0)
    grid = lax.all_gather(grid, "chan", axis=0, tiled=False)

    each = -(-27 // n_dom)
    latent, message = conv_layer(chan[None], grid, wf, wb, inner, outer * each)
    message = exchange(message, "dom", same_x)
    own, rows = width * half, each * CHUNK
    shape = (outer, inner * own + rows, depth)
    message = in_vmem(functools.partial(relay_kernel, own), "relay", shape, message)
    columns = exchange(message, "dom", same_z)

    kgrad = in_vmem(share_kernel, "share", (2 * n_slab, rows, depth), columns)
    kgrad = exchange(kgrad, ("slab", "chan"))
    shape = (n_dom, 2, rows, depth)
    kgrad = in_vmem(functools.partial(finish_kernel, scale), "finish", shape, kgrad)
    kgrad = exchange(kgrad, "dom")
    feature_grad = spread(tile_target, columns, blocks, half, inner * width)
    kgrad, feature_grad = lax.optimization_barrier((kgrad, feature_grad))
    kernel_grad = unpack(kgrad, 27, full, inner)
    return (latent, feature_grad, kernel_grad)


def solution(mesh):
    placed = (
        P("chan", ("dom", "slab")),
        P(None, ("dom", "slab")),
        P(None, ("dom", "slab")),
        P(("dom", "slab")),
        P(("dom", "slab")),
        P(),
        P("chan", "slab", "dom", None),
    )
    return jax.shard_map(
        body,
        mesh=mesh,
        in_specs=placed,
        out_specs=(P("chan", "slab", "dom", None), P("chan", ("dom", "slab")), P()),
        check_vma=False,
    )
```

```python
import functools

import jax
import jax.numpy as jnp
from jax import lax
from jax.experimental import pallas as pl
from jax.experimental.pallas import tpu as pltpu
from jax.sharding import PartitionSpec as P

POOL_GROUP = 32
SPREAD_GROUP = 16
POOL_VMEM = 60 * 1024 * 1024
VMEM_LIMIT = 16 * 1024 * 1024
CHUNK = 16


def cost(flops, moved):
    return pl.CostEstimate(flops=flops, bytes_accessed=moved, transcendentals=0)


def pool_kernel(target, live, cells, weights, feats, blocks, send, acc):
    step = pl.program_id(0)
    tile = blocks.shape[2]
    depth = blocks.shape[1]

    @pl.when(step == 0)
    def _():
        acc[...] = jnp.zeros_like(acc)

    span = cells.shape[1]
    position = step * span + lax.broadcasted_iota(jnp.int32, cells.shape, 1)
    masked = jnp.where(position < live[0], weights[...], 0.0)
    cell = cells[...].astype(jnp.float32)
    depth_ids = lax.broadcasted_iota(jnp.int32, (depth, tile), 0)
    depth_ids = depth_ids.astype(jnp.float32).astype(jnp.bfloat16)

    def spread_rows(row):
        return jnp.broadcast_to(row, (depth, tile)).astype(jnp.bfloat16)

    for t in range(span // tile):
        cols = slice(t * tile, (t + 1) * tile)
        terms = []
        for k in range(cells.shape[0]):
            weight = spread_rows(masked[k : k + 1, cols])
            here = spread_rows(cell[k : k + 1, cols]) == depth_ids
            terms.append(jnp.where(here, weight, jnp.zeros_like(weight)))
        while len(terms) > 1:
            terms = [one + two for one, two in zip(terms[::2], terms[1::2])]
        block = terms[0]
        blocks[t] = block
        part = lax.dot_general(
            feats[:, cols], block, (((1,), (1,)), ((), ())), preferred_element_type=jnp.float32
        )
        column = target[step * (span // tile) + t]
        acc[column] = acc[column] + part

    @pl.when(step == pl.num_programs(0) - 1)
    def _():
        send[...] = acc[...].astype(jnp.bfloat16)


def pool(target, live, cells, weights, feats, n_columns, depth):
    nbrs, npts = cells.shape
    half = feats.shape[0]
    tiles = target.shape[0]
    tile = npts // tiles
    group = min(POOL_GROUP, tiles)
    span = group * tile
    smem = pl.BlockSpec(memory_space=pltpu.SMEM)
    return pl.pallas_call(
        pool_kernel,
        grid=(tiles // group,),
        in_specs=[
            smem,
            smem,
            pl.BlockSpec((nbrs, span), lambda i: (0, i)),
            pl.BlockSpec((nbrs, span), lambda i: (0, i)),
            pl.BlockSpec((half, span), lambda i: (0, i)),
        ],
        out_specs=[
            pl.BlockSpec((group, depth, tile), lambda i: (i, 0, 0)),
            pl.BlockSpec((n_columns, half, depth), lambda i: (0, 0, 0)),
        ],
        out_shape=[
            jax.ShapeDtypeStruct((tiles, depth, tile), jnp.bfloat16),
            jax.ShapeDtypeStruct((n_columns, half, depth), jnp.bfloat16),
        ],
        scratch_shapes=[pltpu.VMEM((n_columns, half, depth), jnp.float32)],
        compiler_params=pltpu.CompilerParams(vmem_limit_bytes=POOL_VMEM),
        cost_estimate=cost(2 * half * npts * depth, 24 * nbrs * npts * depth // 8),
        name="pool",
    )(target, live, cells, weights, feats)


def spread_kernel(target, place, *refs):
    *parts, blocks, out, columns = refs
    step = pl.program_id(0)
    group, _, tile = blocks.shape
    count = parts[0].shape[0]

    @pl.when(step == 0)
    def _():
        shift = 0
        for part in parts:
            for first in range(0, part.shape[0], count):
                source = jnp.bitwise_xor(place[0], shift)
                columns[pl.ds(source * count, count)] = part[first : first + count]
                shift += 1

    for t in range(group):
        column = target[step * group + t]
        value = jnp.dot(columns[column], blocks[t], preferred_element_type=jnp.float32)
        out[:, t * tile : (t + 1) * tile] = value.astype(jnp.bfloat16)


def spread(target, place, parts, blocks):
    tiles, depth, tile = blocks.shape
    half = parts[0].shape[1]
    group = min(SPREAD_GROUP, tiles)
    smem = pl.BlockSpec(memory_space=pltpu.SMEM)
    total = sum(part.shape[0] for part in parts)
    return pl.pallas_call(
        spread_kernel,
        grid=(tiles // group,),
        in_specs=[smem, smem]
        + [pl.BlockSpec(part.shape, lambda i: (0, 0, 0)) for part in parts]
        + [pl.BlockSpec((group, depth, tile), lambda i: (i, 0, 0))],
        out_specs=pl.BlockSpec((half, group * tile), lambda i: (0, i)),
        out_shape=jax.ShapeDtypeStruct((half, tiles * tile), jnp.bfloat16),
        scratch_shapes=[pltpu.VMEM((total, half, depth), jnp.bfloat16)],
        compiler_params=pltpu.CompilerParams(vmem_limit_bytes=VMEM_LIMIT),
        cost_estimate=cost(2 * half * tiles * tile * depth, 6 * tiles * tile * depth),
        name="spread",
    )(target, place, *parts, blocks)


def in_vmem(kernel, name, out_shape, *args):
    vmem = pl.BlockSpec(memory_space=pltpu.VMEM)
    return pl.pallas_call(
        kernel,
        in_specs=[vmem] * len(args),
        out_specs=vmem,
        out_shape=jax.ShapeDtypeStruct(out_shape, jnp.bfloat16),
        compiler_params=pltpu.CompilerParams(vmem_limit_bytes=VMEM_LIMIT),
        name=name,
    )(*args)


def added(parts):
    total = parts[0].astype(jnp.float32)
    for part in parts[1:]:
        total = total + part.astype(jnp.float32)
    return total


def add_kernel(received, out):
    count = out.shape[0]
    for d in range(count):
        parts = [received[first + d] for first in range(0, received.shape[0], count)]
        out[d] = added(parts).astype(jnp.bfloat16)


def split_kernel(received, columns, message):
    sources, own, _ = columns.shape
    outer, peers, rows, _ = message.shape
    total = added([received[z, own:, :] for z in range(sources)]).astype(jnp.bfloat16)
    for z in range(sources):
        columns[z] = received[z, :own, :]
    for x in range(outer):
        for peer in range(peers):
            message[x, peer] = total[x * rows : (x + 1) * rows]


def split(received, own, outer, peers):
    sources, rows, depth = received.shape
    vmem = pl.BlockSpec(memory_space=pltpu.VMEM)
    return pl.pallas_call(
        split_kernel,
        in_specs=[vmem],
        out_specs=[vmem, vmem],
        out_shape=[
            jax.ShapeDtypeStruct((sources, own, depth), jnp.bfloat16),
            jax.ShapeDtypeStruct((outer, peers, (rows - own) // outer, depth), jnp.bfloat16),
        ],
        compiler_params=pltpu.CompilerParams(vmem_limit_bytes=VMEM_LIMIT),
        name="split",
    )(received)


def finish_kernel(scale, received, message):
    for c in range(2):
        total = added([received[s + c] for s in range(0, received.shape[0], 2)]) * scale
        total = total.astype(jnp.bfloat16)
        for peer in range(message.shape[0]):
            message[peer, c] = total


def unpack_kernel(inner, gathered, out):
    n_dom = gathered.shape[0]
    outer = n_dom // inner
    half = out.shape[2] // 2
    each = gathered.shape[2] // CHUNK
    for k in range(out.shape[0]):
        place = k // each
        source = place % outer * inner + place // outer
        rows = slice(k % each * CHUNK, (k % each + 1) * CHUNK)
        first = gathered[source, 0, rows, :].astype(jnp.float32)
        second = gathered[source, 1, rows, :].astype(jnp.float32)
        for g in range(out.shape[1] // CHUNK):
            lanes = slice(g * half, (g + 1) * half)
            out[k, g * CHUNK : (g + 1) * CHUNK, :] = jnp.concatenate(
                [first[:, lanes], second[:, lanes]], 1
            )


def unpack(gathered, offsets, full, inner):
    vmem = pl.BlockSpec(memory_space=pltpu.VMEM)
    return pl.pallas_call(
        functools.partial(unpack_kernel, inner),
        in_specs=[vmem],
        out_specs=vmem,
        out_shape=jax.ShapeDtypeStruct((offsets, full, full), jnp.float32),
        compiler_params=pltpu.CompilerParams(vmem_limit_bytes=VMEM_LIMIT),
        name="unpack",
    )(gathered)


def later(value, lane):
    return jnp.where(lane == 0, 0.0, pltpu.roll(value, 1, 1))


def earlier(value, lane):
    depth = value.shape[1]
    return jnp.where(lane == depth - 1, 0.0, pltpu.roll(value, depth - 1, 1))


def conv_kernel_body(chan, grid, wf, wb, latent, message, pp, dd, hh):
    half, depth = grid.shape[2], grid.shape[3]
    full = 2 * half
    n_dom = message.shape[0]

    def cot(c, y, x):
        return grid[c, (12 + y, 27 + 2 * y + x, 27 + 2 * y + x, 48 + y)[x]]

    per = message.shape[1] // CHUNK - 4 * half // CHUNK
    first = pl.multiple_of(chan[0] * half, half)
    for s in range(3):
        for y in range(6):
            for x in range(2):
                for c in range(2):
                    rows = slice(y * full + c * half, y * full + (c + 1) * half)
                    pp[2 * s + x, rows, :] = grid[c, (0, 16, 36)[s] + 2 * y + x]
    lane = lax.broadcasted_iota(jnp.int32, (full, depth), 1)
    for x in range(4):
        for y in range(4):
            grown = jnp.zeros((3 * full, depth), jnp.float32)
            for a in range(3):
                grown = grown + jnp.dot(
                    wf[a],
                    pp[x + a, y * full : (y + 3) * full, :],
                    preferred_element_type=jnp.float32,
                )
            h = (
                grown[full : 2 * full]
                + later(grown[:full], lane)
                + earlier(grown[2 * full :], lane)
            )
            sig = jax.nn.sigmoid(h)
            upper = jnp.concatenate([cot(0, y, x), cot(1, y, x)], 0).astype(jnp.float32)
            dd[x, y * full : (y + 1) * full, :] = (upper * sig * (1.0 + h * (1.0 - sig))).astype(
                jnp.bfloat16
            )
            if x in (1, 2) and y in (1, 2):
                hh[...] = h * sig
                mine = pp[x + 1, pl.ds((y + 1) * full + first, half), :].astype(jnp.float32)
                latent[:, x - 1, y - 1, :] = (mine + hh[pl.ds(first, half), :]).astype(jnp.bfloat16)
    lane = lax.broadcasted_iota(jnp.int32, (half, depth), 1)
    for x in range(2):
        for y in range(2):
            grown = jnp.zeros((3 * half, depth), jnp.float32)
            for a in range(3):
                grown = grown + jnp.dot(
                    wb[a],
                    dd[x + a, y * full : (y + 3) * full, :],
                    preferred_element_type=jnp.float32,
                )
            dx = (
                grown[half : 2 * half]
                + earlier(grown[:half], lane)
                + later(grown[2 * half :], lane)
            )
            own = cot(chan[0], y + 1, x + 1).astype(jnp.float32)
            column = (own + dx).astype(jnp.bfloat16)
            for d in range(n_dom):
                message[d, (2 * y + x) * half : (2 * y + x + 1) * half, :] = column
    moved = []
    for x in range(2):
        for y in range(2):
            own = dd[x + 1, pl.ds((y + 1) * full + first, half), :].astype(jnp.float32)
            moved.append(
                jnp.concatenate(
                    [earlier(own, lane), own, later(own, lane), jnp.zeros_like(own)], 0
                ).astype(jnp.bfloat16)
            )
    for a in range(3):
        total = jnp.zeros((3 * full, 4 * half), jnp.float32)
        for x in range(2):
            for y in range(2):
                total = total + lax.dot_general(
                    pp[x + 1 + a, (y + 1) * full : (y + 4) * full, :],
                    moved[2 * x + y],
                    (((1,), (1,)), ((), ())),
                    preferred_element_type=jnp.float32,
                )
        for b in range(3):
            for e in range(3):
                k = 9 * a + 3 * b + e
                pieces = [
                    total[b * full + g * CHUNK : b * full + (g + 1) * CHUNK, e * half : (e + 1) * half]
                    for g in range(full // CHUNK)
                ]
                row = 4 * half + k % per * CHUNK
                message[k // per, row : row + CHUNK, :] = jnp.concatenate(pieces, 1).astype(
                    jnp.bfloat16
                )
    for k in range(27, n_dom * per):
        row = 4 * half + k % per * CHUNK
        message[k // per, row : row + CHUNK, :] = jnp.zeros((CHUNK, depth), jnp.bfloat16)


def conv_layer(chan, grid, wf, wb, n_dom, per):
    half, depth = grid.shape[2], grid.shape[3]
    full = 2 * half
    vmem = pl.BlockSpec(memory_space=pltpu.VMEM)
    return pl.pallas_call(
        conv_kernel_body,
        in_specs=[pl.BlockSpec(memory_space=pltpu.SMEM), vmem, vmem, vmem],
        out_specs=[vmem, vmem],
        out_shape=[
            jax.ShapeDtypeStruct((half, 2, 2, depth), jnp.bfloat16),
            jax.ShapeDtypeStruct((n_dom, 4 * half + per * CHUNK, depth), jnp.bfloat16),
        ],
        scratch_shapes=[
            pltpu.VMEM((6, 6 * full, depth), jnp.bfloat16),
            pltpu.VMEM((4, 4 * full, depth), jnp.bfloat16),
            pltpu.VMEM((full, depth), jnp.float32),
        ],
        compiler_params=pltpu.CompilerParams(vmem_limit_bytes=VMEM_LIMIT),
        name="conv_layer",
    )(chan, grid, wf, wb)


def neighbours(first, last, axis):
    peers = lax.axis_size(axis)
    up = [(i, i + 1) for i in range(peers - 1)]
    down = [(j, i) for i, j in up]
    return lax.ppermute(last, axis, up), lax.ppermute(first, axis, down)


def paired(groups, shift):
    return [(group[i], group[i ^ shift]) for group in groups for i in range(len(group))]


def body(
    point_features,
    neighbour_cells,
    neighbour_weights,
    live_points,
    tile_target,
    conv_kernel,
    cotangent,
):
    half = point_features.shape[0]
    full = 2 * half
    xsize, ysize, depth = cotangent.shape[1:]
    n_dom, n_slab = lax.axis_size("dom"), lax.axis_size("slab")
    width = xsize * ysize
    chan = lax.axis_index("chan").astype(jnp.int32)
    scale = float(width * depth * n_dom * n_slab) ** (-0.5)

    blocks, send = pool(
        tile_target,
        live_points,
        neighbour_cells,
        neighbour_weights,
        point_features,
        n_dom * width,
        depth,
    )

    kernel = conv_kernel.reshape(3, 3, 3, full, full)
    wf = kernel.transpose(0, 2, 4, 1, 3).reshape(3, 3 * full, 3 * full)
    wb = lax.dynamic_slice_in_dim(kernel[::-1, ::-1], chan * half, half, 3)
    wb = wb.transpose(0, 2, 3, 1, 4).reshape(3, 3 * half, 3 * full)

    inner = min(8, n_dom // 2)
    outer = n_dom // inner
    same_z = [[x * inner + z for x in range(outer)] for z in range(inner)]
    same_x = [[x * inner + z for z in range(inner)] for x in range(outer)]

    def exchange(value, axis, groups=None):
        return lax.all_to_all(
            value, axis, split_axis=0, concat_axis=0, tiled=True, axis_index_groups=groups
        )

    def total(value, parts):
        return value.reshape((parts, -1) + value.shape[1:]).astype(jnp.float32).sum(0)

    part = exchange(send, "dom", same_z)
    part = in_vmem(add_kernel, "add_x", (part.shape[0] // outer,) + part.shape[1:], part)
    part = exchange(part, "dom", same_x)
    part, wf, wb = lax.optimization_barrier((part, wf, wb))
    pooled = total(part, inner).astype(jnp.bfloat16)

    cot = cotangent.transpose(2, 1, 0, 3)
    before, after = neighbours(
        jnp.concatenate([pooled, cot[0]], 0), jnp.concatenate([pooled, cot[-1]], 0), "dom"
    )
    pooled = jnp.concatenate([before[:width], pooled, after[:width]], 0)
    cot = jnp.concatenate([before[None, width:], cot, after[None, width:]], 0)
    before, after = neighbours(
        jnp.concatenate([pooled, cot[:, 0]], 0), jnp.concatenate([pooled, cot[:, -1]], 0), "slab"
    )
    grid = jnp.concatenate([before, pooled, cot.reshape((-1,) + cot.shape[2:]), after], 0)
    grid = lax.all_gather(grid, "chan", axis=0, tiled=False)

    each = -(-27 // n_dom)
    latent, message = conv_layer(chan[None], grid, wf, wb, inner, outer * each)
    message = exchange(message, "dom", same_x)
    peers, rows = 2 * n_slab, each * CHUNK
    columns, kgrad = split(message, width * half, outer, peers)

    same_z_all = [
        [(x * inner + z) * peers + p for x in range(outer) for p in range(peers)]
        for z in range(inner)
    ]
    columns = columns.reshape(inner * width, half, depth)
    parts = [columns, lax.ppermute(columns, "dom", paired(same_z, 1))]
    kgrad = exchange(
        kgrad.reshape(outer * peers, rows, depth), ("dom", "slab", "chan"), same_z_all
    )
    shape = (n_dom, 2, rows, depth)
    kgrad = in_vmem(functools.partial(finish_kernel, scale), "finish", shape, kgrad)
    kgrad, parts = lax.optimization_barrier((kgrad, parts))
    kgrad = exchange(kgrad, "dom")
    shift = 2
    while shift < outer:
        parts.append(lax.ppermute(jnp.concatenate(parts, 0), "dom", paired(same_z, shift)))
        shift = 2 * shift
    place = (lax.axis_index("dom") // inner).astype(jnp.int32)
    feature_grad = spread(tile_target, place[None], parts, blocks)
    kgrad, feature_grad = lax.optimization_barrier((kgrad, feature_grad))
    kernel_grad = unpack(kgrad, 27, full, inner)
    return (latent, feature_grad, kernel_grad)


def solution(mesh):
    placed = (
        P("chan", ("dom", "slab")),
        P(None, ("dom", "slab")),
        P(None, ("dom", "slab")),
        P(("dom", "slab")),
        P(("dom", "slab")),
        P(),
        P("chan", "slab", "dom", None),
    )
    return jax.shard_map(
        body,
        mesh=mesh,
        in_specs=placed,
        out_specs=(P("chan", "slab", "dom", None), P("chan", ("dom", "slab")), P()),
        check_vma=False,
    )
```

```python
import functools

import jax
import jax.numpy as jnp
from jax import lax
from jax.experimental import pallas as pl
from jax.experimental.pallas import tpu as pltpu
from jax.sharding import PartitionSpec as P

POOL_GROUP = 32
SPREAD_GROUP = 16
POOL_VMEM = 60 * 1024 * 1024
VMEM_LIMIT = 16 * 1024 * 1024
CHUNK = 16


def cost(flops, moved):
    return pl.CostEstimate(flops=flops, bytes_accessed=moved, transcendentals=0)


def pool_kernel(target, live, cells, weights, feats, blocks, send, acc):
    step = pl.program_id(0)
    tile = blocks.shape[2]
    depth = blocks.shape[1]

    @pl.when(step == 0)
    def _():
        acc[...] = jnp.zeros_like(acc)

    span = cells.shape[1]
    position = step * span + lax.broadcasted_iota(jnp.int32, cells.shape, 1)
    masked = jnp.where(position < live[0], weights[...], 0.0)
    cell = cells[...].astype(jnp.float32)
    depth_ids = lax.broadcasted_iota(jnp.int32, (depth, tile), 0)
    depth_ids = depth_ids.astype(jnp.float32).astype(jnp.bfloat16)

    def spread_rows(row):
        return jnp.broadcast_to(row, (depth, tile)).astype(jnp.bfloat16)

    for t in range(span // tile):
        cols = slice(t * tile, (t + 1) * tile)
        terms = []
        for k in range(cells.shape[0]):
            weight = spread_rows(masked[k : k + 1, cols])
            here = spread_rows(cell[k : k + 1, cols]) == depth_ids
            terms.append(jnp.where(here, weight, jnp.zeros_like(weight)))
        while len(terms) > 1:
            terms = [one + two for one, two in zip(terms[::2], terms[1::2])]
        block = terms[0]
        blocks[t] = block
        part = lax.dot_general(
            feats[:, cols], block, (((1,), (1,)), ((), ())), preferred_element_type=jnp.float32
        )
        column = target[step * (span // tile) + t]
        acc[column] = acc[column] + part

    @pl.when(step == pl.num_programs(0) - 1)
    def _():
        send[...] = acc[...].astype(jnp.bfloat16)


def pool(target, live, cells, weights, feats, n_columns, depth):
    nbrs, npts = cells.shape
    half = feats.shape[0]
    tiles = target.shape[0]
    tile = npts // tiles
    group = min(POOL_GROUP, tiles)
    span = group * tile
    smem = pl.BlockSpec(memory_space=pltpu.SMEM)
    return pl.pallas_call(
        pool_kernel,
        grid=(tiles // group,),
        in_specs=[
            smem,
            smem,
            pl.BlockSpec((nbrs, span), lambda i: (0, i)),
            pl.BlockSpec((nbrs, span), lambda i: (0, i)),
            pl.BlockSpec((half, span), lambda i: (0, i)),
        ],
        out_specs=[
            pl.BlockSpec((group, depth, tile), lambda i: (i, 0, 0)),
            pl.BlockSpec((n_columns, half, depth), lambda i: (0, 0, 0)),
        ],
        out_shape=[
            jax.ShapeDtypeStruct((tiles, depth, tile), jnp.bfloat16),
            jax.ShapeDtypeStruct((n_columns, half, depth), jnp.bfloat16),
        ],
        scratch_shapes=[pltpu.VMEM((n_columns, half, depth), jnp.float32)],
        compiler_params=pltpu.CompilerParams(vmem_limit_bytes=POOL_VMEM),
        cost_estimate=cost(2 * half * npts * depth, 24 * nbrs * npts * depth // 8),
        name="pool",
    )(target, live, cells, weights, feats)


def spread_kernel(target, place, *refs):
    *parts, blocks, out, columns = refs
    step = pl.program_id(0)
    group, _, tile = blocks.shape
    count = parts[0].shape[0]

    @pl.when(step == 0)
    def _():
        shift = 0
        for part in parts:
            for first in range(0, part.shape[0], count):
                source = jnp.bitwise_xor(place[0], shift)
                columns[pl.ds(source * count, count)] = part[first : first + count]
                shift += 1

    for t in range(group):
        column = target[step * group + t]
        value = jnp.dot(columns[column], blocks[t], preferred_element_type=jnp.float32)
        out[:, t * tile : (t + 1) * tile] = value.astype(jnp.bfloat16)


def spread(target, place, parts, blocks):
    tiles, depth, tile = blocks.shape
    half = parts[0].shape[1]
    group = min(SPREAD_GROUP, tiles)
    smem = pl.BlockSpec(memory_space=pltpu.SMEM)
    total = sum(part.shape[0] for part in parts)
    return pl.pallas_call(
        spread_kernel,
        grid=(tiles // group,),
        in_specs=[smem, smem]
        + [pl.BlockSpec(part.shape, lambda i: (0, 0, 0)) for part in parts]
        + [pl.BlockSpec((group, depth, tile), lambda i: (i, 0, 0))],
        out_specs=pl.BlockSpec((half, group * tile), lambda i: (0, i)),
        out_shape=jax.ShapeDtypeStruct((half, tiles * tile), jnp.bfloat16),
        scratch_shapes=[pltpu.VMEM((total, half, depth), jnp.bfloat16)],
        compiler_params=pltpu.CompilerParams(vmem_limit_bytes=VMEM_LIMIT),
        cost_estimate=cost(2 * half * tiles * tile * depth, 6 * tiles * tile * depth),
        name="spread",
    )(target, place, *parts, blocks)


def in_vmem(kernel, name, out_shape, *args):
    vmem = pl.BlockSpec(memory_space=pltpu.VMEM)
    return pl.pallas_call(
        kernel,
        in_specs=[vmem] * len(args),
        out_specs=vmem,
        out_shape=jax.ShapeDtypeStruct(out_shape, jnp.bfloat16),
        compiler_params=pltpu.CompilerParams(vmem_limit_bytes=VMEM_LIMIT),
        name=name,
    )(*args)


def added(parts):
    total = parts[0].astype(jnp.float32)
    for part in parts[1:]:
        total = total + part.astype(jnp.float32)
    return total


def add_kernel(received, out):
    count = out.shape[0]
    for d in range(count):
        parts = [received[first + d] for first in range(0, received.shape[0], count)]
        out[d] = added(parts).astype(jnp.bfloat16)


def split_kernel(received, columns, message):
    sources, own, _ = columns.shape
    outer, peers, rows, _ = message.shape
    total = added([received[z, own:, :] for z in range(sources)]).astype(jnp.bfloat16)
    for z in range(sources):
        columns[z] = received[z, :own, :]
    for x in range(outer):
        for peer in range(peers):
            message[x, peer] = total[x * rows : (x + 1) * rows]


def split(received, own, outer, peers):
    sources, rows, depth = received.shape
    vmem = pl.BlockSpec(memory_space=pltpu.VMEM)
    return pl.pallas_call(
        split_kernel,
        in_specs=[vmem],
        out_specs=[vmem, vmem],
        out_shape=[
            jax.ShapeDtypeStruct((sources, own, depth), jnp.bfloat16),
            jax.ShapeDtypeStruct((outer, peers, (rows - own) // outer, depth), jnp.bfloat16),
        ],
        compiler_params=pltpu.CompilerParams(vmem_limit_bytes=VMEM_LIMIT),
        name="split",
    )(received)


def finish_kernel(scale, received, message):
    for c in range(2):
        total = added([received[s + c] for s in range(0, received.shape[0], 2)]) * scale
        total = total.astype(jnp.bfloat16)
        for peer in range(message.shape[0]):
            message[peer, c] = total


def unpack_kernel(inner, gathered, out):
    n_dom = gathered.shape[0]
    outer = n_dom // inner
    half = out.shape[2] // 2
    each = gathered.shape[2] // CHUNK
    for k in range(out.shape[0]):
        place = k // each
        source = place % outer * inner + place // outer
        rows = slice(k % each * CHUNK, (k % each + 1) * CHUNK)
        first = gathered[source, 0, rows, :].astype(jnp.float32)
        second = gathered[source, 1, rows, :].astype(jnp.float32)
        for g in range(out.shape[1] // CHUNK):
            lanes = slice(g * half, (g + 1) * half)
            out[k, g * CHUNK : (g + 1) * CHUNK, :] = jnp.concatenate(
                [first[:, lanes], second[:, lanes]], 1
            )


def unpack(gathered, offsets, full, inner):
    vmem = pl.BlockSpec(memory_space=pltpu.VMEM)
    return pl.pallas_call(
        functools.partial(unpack_kernel, inner),
        in_specs=[vmem],
        out_specs=vmem,
        out_shape=jax.ShapeDtypeStruct((offsets, full, full), jnp.float32),
        compiler_params=pltpu.CompilerParams(vmem_limit_bytes=VMEM_LIMIT),
        name="unpack",
    )(gathered)


def later(value, lane):
    return jnp.where(lane == 0, 0.0, pltpu.roll(value, 1, 1))


def earlier(value, lane):
    depth = value.shape[1]
    return jnp.where(lane == depth - 1, 0.0, pltpu.roll(value, depth - 1, 1))


def wide_products(weights, values, size, full):
    depth = values.shape[2]
    for x in range(size):
        for y in range(0, size, 2):
            total = None
            for a in range(3):
                window = jnp.concatenate(
                    [values[x + a, (y + i) * full : (y + i + 3) * full, :] for i in range(2)], 1
                )
                product = jnp.dot(weights[a], window, preferred_element_type=jnp.float32)
                total = product if total is None else total + product
            for i in range(2):
                yield x, y + i, total[:, i * depth : (i + 1) * depth]


def conv_kernel_body(chan, grid, wf, wb, latent, message, pp, dd, hh):
    half, depth = grid.shape[2], grid.shape[3]
    full = 2 * half
    n_dom = message.shape[0]

    def cot(c, y, x):
        return grid[c, (12 + y, 27 + 2 * y + x, 27 + 2 * y + x, 48 + y)[x]]

    per = message.shape[1] // CHUNK - 4 * half // CHUNK
    first = pl.multiple_of(chan[0] * half, half)
    for s in range(3):
        for y in range(6):
            for x in range(2):
                for c in range(2):
                    rows = slice(y * full + c * half, y * full + (c + 1) * half)
                    pp[2 * s + x, rows, :] = grid[c, (0, 16, 36)[s] + 2 * y + x]
    lane = lax.broadcasted_iota(jnp.int32, (full, depth), 1)
    for x, y, grown in wide_products(wf, pp, 4, full):
        h = (
            grown[full : 2 * full]
            + later(grown[:full], lane)
            + earlier(grown[2 * full :], lane)
        )
        sig = jax.nn.sigmoid(h)
        upper = jnp.concatenate([cot(0, y, x), cot(1, y, x)], 0).astype(jnp.float32)
        dd[x, y * full : (y + 1) * full, :] = (upper * sig * (1.0 + h * (1.0 - sig))).astype(
            jnp.bfloat16
        )
        if x in (1, 2) and y in (1, 2):
            hh[...] = h * sig
            mine = pp[x + 1, pl.ds((y + 1) * full + first, half), :].astype(jnp.float32)
            latent[:, x - 1, y - 1, :] = (mine + hh[pl.ds(first, half), :]).astype(jnp.bfloat16)
    lane = lax.broadcasted_iota(jnp.int32, (half, depth), 1)
    for x, y, grown in wide_products(wb, dd, 2, full):
        dx = (
            grown[half : 2 * half]
            + earlier(grown[:half], lane)
            + later(grown[2 * half :], lane)
        )
        own = cot(chan[0], y + 1, x + 1).astype(jnp.float32)
        column = (own + dx).astype(jnp.bfloat16)
        for d in range(n_dom):
            message[d, (2 * y + x) * half : (2 * y + x + 1) * half, :] = column
    moved = []
    for x in range(2):
        for y in range(2):
            own = dd[x + 1, pl.ds((y + 1) * full + first, half), :].astype(jnp.float32)
            moved.append(
                jnp.concatenate(
                    [earlier(own, lane), own, later(own, lane), jnp.zeros_like(own)], 0
                ).astype(jnp.bfloat16)
            )
    moved = jnp.concatenate(moved, 1)
    for a in range(3):
        windows = [
            pp[x + 1 + a, (y + 1) * full : (y + 4) * full, :] for x in range(2) for y in range(2)
        ]
        total = lax.dot_general(
            jnp.concatenate(windows, 1),
            moved,
            (((1,), (1,)), ((), ())),
            preferred_element_type=jnp.float32,
        )
        for b in range(3):
            for e in range(3):
                k = 9 * a + 3 * b + e
                pieces = [
                    total[b * full + g * CHUNK : b * full + (g + 1) * CHUNK, e * half : (e + 1) * half]
                    for g in range(full // CHUNK)
                ]
                row = 4 * half + k % per * CHUNK
                message[k // per, row : row + CHUNK, :] = jnp.concatenate(pieces, 1).astype(
                    jnp.bfloat16
                )
    for k in range(27, n_dom * per):
        row = 4 * half + k % per * CHUNK
        message[k // per, row : row + CHUNK, :] = jnp.zeros((CHUNK, depth), jnp.bfloat16)


def conv_layer(chan, grid, wf, wb, n_dom, per):
    half, depth = grid.shape[2], grid.shape[3]
    full = 2 * half
    vmem = pl.BlockSpec(memory_space=pltpu.VMEM)
    return pl.pallas_call(
        conv_kernel_body,
        in_specs=[pl.BlockSpec(memory_space=pltpu.SMEM), vmem, vmem, vmem],
        out_specs=[vmem, vmem],
        out_shape=[
            jax.ShapeDtypeStruct((half, 2, 2, depth), jnp.bfloat16),
            jax.ShapeDtypeStruct((n_dom, 4 * half + per * CHUNK, depth), jnp.bfloat16),
        ],
        scratch_shapes=[
            pltpu.VMEM((6, 6 * full, depth), jnp.bfloat16),
            pltpu.VMEM((4, 4 * full, depth), jnp.bfloat16),
            pltpu.VMEM((full, depth), jnp.float32),
        ],
        compiler_params=pltpu.CompilerParams(vmem_limit_bytes=VMEM_LIMIT),
        name="conv_layer",
    )(chan, grid, wf, wb)


def neighbours(first, last, axis):
    peers = lax.axis_size(axis)
    up = [(i, i + 1) for i in range(peers - 1)]
    down = [(j, i) for i, j in up]
    return lax.ppermute(last, axis, up), lax.ppermute(first, axis, down)


def paired(groups, shift):
    return [(group[i], group[i ^ shift]) for group in groups for i in range(len(group))]


def body(
    point_features,
    neighbour_cells,
    neighbour_weights,
    live_points,
    tile_target,
    conv_kernel,
    cotangent,
):
    half = point_features.shape[0]
    full = 2 * half
    xsize, ysize, depth = cotangent.shape[1:]
    n_dom, n_slab = lax.axis_size("dom"), lax.axis_size("slab")
    width = xsize * ysize
    chan = lax.axis_index("chan").astype(jnp.int32)
    scale = float(width * depth * n_dom * n_slab) ** (-0.5)

    blocks, send = pool(
        tile_target,
        live_points,
        neighbour_cells,
        neighbour_weights,
        point_features,
        n_dom * width,
        depth,
    )

    kernel = conv_kernel.reshape(3, 3, 3, full, full)
    wf = kernel.transpose(0, 2, 4, 1, 3).reshape(3, 3 * full, 3 * full)
    wb = lax.dynamic_slice_in_dim(kernel[::-1, ::-1], chan * half, half, 3)
    wb = wb.transpose(0, 2, 3, 1, 4).reshape(3, 3 * half, 3 * full)

    inner = min(8, n_dom // 2)
    outer = n_dom // inner
    same_z = [[x * inner + z for x in range(outer)] for z in range(inner)]
    same_x = [[x * inner + z for z in range(inner)] for x in range(outer)]

    def exchange(value, axis, groups=None):
        return lax.all_to_all(
            value, axis, split_axis=0, concat_axis=0, tiled=True, axis_index_groups=groups
        )

    def total(value, parts):
        return value.reshape((parts, -1) + value.shape[1:]).astype(jnp.float32).sum(0)

    part = exchange(send, "dom", same_z)
    part = in_vmem(add_kernel, "add_x", (part.shape[0] // outer,) + part.shape[1:], part)
    part = exchange(part, "dom", same_x)
    part, wf, wb = lax.optimization_barrier((part, wf, wb))
    pooled = total(part, inner).astype(jnp.bfloat16)

    cot = cotangent.transpose(2, 1, 0, 3)
    before, after = neighbours(
        jnp.concatenate([pooled, cot[0]], 0), jnp.concatenate([pooled, cot[-1]], 0), "dom"
    )
    pooled = jnp.concatenate([before[:width], pooled, after[:width]], 0)
    cot = jnp.concatenate([before[None, width:], cot, after[None, width:]], 0)
    before, after = neighbours(
        jnp.concatenate([pooled, cot[:, 0]], 0), jnp.concatenate([pooled, cot[:, -1]], 0), "slab"
    )
    grid = jnp.concatenate([before, pooled, cot.reshape((-1,) + cot.shape[2:]), after], 0)
    grid = lax.all_gather(grid, "chan", axis=0, tiled=False)

    each = -(-27 // n_dom)
    latent, message = conv_layer(chan[None], grid, wf, wb, inner, outer * each)
    message = exchange(message, "dom", same_x)
    peers, rows = 2 * n_slab, each * CHUNK
    columns, kgrad = split(message, width * half, outer, peers)

    same_z_all = [
        [(x * inner + z) * peers + p for x in range(outer) for p in range(peers)]
        for z in range(inner)
    ]
    columns = columns.reshape(inner * width, half, depth)
    parts = [columns, lax.ppermute(columns, "dom", paired(same_z, 1))]
    kgrad = exchange(
        kgrad.reshape(outer * peers, rows, depth), ("dom", "slab", "chan"), same_z_all
    )
    shape = (n_dom, 2, rows, depth)
    kgrad = in_vmem(functools.partial(finish_kernel, scale), "finish", shape, kgrad)
    kgrad = exchange(kgrad, "dom")
    shift = 2
    while shift < outer:
        parts.append(lax.ppermute(jnp.concatenate(parts, 0), "dom", paired(same_z, shift)))
        shift = 2 * shift
    place = (lax.axis_index("dom") // inner).astype(jnp.int32)
    feature_grad = spread(tile_target, place[None], parts, blocks)
    kgrad, feature_grad = lax.optimization_barrier((kgrad, feature_grad))
    kernel_grad = unpack(kgrad, 27, full, inner)
    return (latent, feature_grad, kernel_grad)


def solution(mesh):
    placed = (
        P("chan", ("dom", "slab")),
        P(None, ("dom", "slab")),
        P(None, ("dom", "slab")),
        P(("dom", "slab")),
        P(("dom", "slab")),
        P(),
        P("chan", "slab", "dom", None),
    )
    return jax.shard_map(
        body,
        mesh=mesh,
        in_specs=placed,
        out_specs=(P("chan", "slab", "dom", None), P("chan", ("dom", "slab")), P()),
        check_vma=False,
    )
```

```python
import functools

import jax
import jax.numpy as jnp
from jax import lax
from jax.experimental import pallas as pl
from jax.experimental.pallas import tpu as pltpu
from jax.sharding import PartitionSpec as P

POOL_GROUP = 32
SPREAD_GROUP = 16
POOL_VMEM = 60 * 1024 * 1024
VMEM_LIMIT = 16 * 1024 * 1024
CHUNK = 16


def cost(flops, moved):
    return pl.CostEstimate(flops=flops, bytes_accessed=moved, transcendentals=0)


def pool_kernel(target, live, cells, weights, feats, blocks, send, acc):
    step = pl.program_id(0)
    tile = blocks.shape[2]
    depth = blocks.shape[1]

    @pl.when(step == 0)
    def _():
        acc[...] = jnp.zeros_like(acc)

    span = cells.shape[1]
    position = step * span + lax.broadcasted_iota(jnp.int32, cells.shape, 1)
    masked = jnp.where(position < live[0], weights[...], 0.0)
    cell = cells[...].astype(jnp.float32)
    depth_ids = lax.broadcasted_iota(jnp.int32, (depth, tile), 0)
    depth_ids = depth_ids.astype(jnp.float32).astype(jnp.bfloat16)

    def spread_rows(row):
        return jnp.broadcast_to(row, (depth, tile)).astype(jnp.bfloat16)

    for t in range(span // tile):
        cols = slice(t * tile, (t + 1) * tile)
        terms = []
        for k in range(cells.shape[0]):
            weight = spread_rows(masked[k : k + 1, cols])
            here = spread_rows(cell[k : k + 1, cols]) == depth_ids
            terms.append(jnp.where(here, weight, jnp.zeros_like(weight)))
        while len(terms) > 1:
            terms = [one + two for one, two in zip(terms[::2], terms[1::2])]
        block = terms[0]
        blocks[t] = block
        part = lax.dot_general(
            feats[:, cols], block, (((1,), (1,)), ((), ())), preferred_element_type=jnp.float32
        )
        column = target[step * (span // tile) + t]
        acc[column] = acc[column] + part

    @pl.when(step == pl.num_programs(0) - 1)
    def _():
        send[...] = acc[...].astype(jnp.bfloat16)


def pool(target, live, cells, weights, feats, n_columns, depth):
    nbrs, npts = cells.shape
    half = feats.shape[0]
    tiles = target.shape[0]
    tile = npts // tiles
    group = min(POOL_GROUP, tiles)
    span = group * tile
    smem = pl.BlockSpec(memory_space=pltpu.SMEM)
    return pl.pallas_call(
        pool_kernel,
        grid=(tiles // group,),
        in_specs=[
            smem,
            smem,
            pl.BlockSpec((nbrs, span), lambda i: (0, i)),
            pl.BlockSpec((nbrs, span), lambda i: (0, i)),
            pl.BlockSpec((half, span), lambda i: (0, i)),
        ],
        out_specs=[
            pl.BlockSpec((group, depth, tile), lambda i: (i, 0, 0)),
            pl.BlockSpec((n_columns, half, depth), lambda i: (0, 0, 0)),
        ],
        out_shape=[
            jax.ShapeDtypeStruct((tiles, depth, tile), jnp.bfloat16),
            jax.ShapeDtypeStruct((n_columns, half, depth), jnp.bfloat16),
        ],
        scratch_shapes=[pltpu.VMEM((n_columns, half, depth), jnp.float32)],
        compiler_params=pltpu.CompilerParams(vmem_limit_bytes=POOL_VMEM),
        cost_estimate=cost(2 * half * npts * depth, 24 * nbrs * npts * depth // 8),
        name="pool",
    )(target, live, cells, weights, feats)


def spread_kernel(target, place, *refs):
    *parts, blocks, out, columns = refs
    step = pl.program_id(0)
    group, _, tile = blocks.shape
    count = parts[0].shape[0]

    @pl.when(step == 0)
    def _():
        shift = 0
        for part in parts:
            for first in range(0, part.shape[0], count):
                source = jnp.bitwise_xor(place[0], shift)
                columns[pl.ds(source * count, count)] = part[first : first + count]
                shift += 1

    for t in range(group):
        column = target[step * group + t]
        value = jnp.dot(columns[column], blocks[t], preferred_element_type=jnp.float32)
        out[:, t * tile : (t + 1) * tile] = value.astype(jnp.bfloat16)


def spread(target, place, parts, blocks):
    tiles, depth, tile = blocks.shape
    half = parts[0].shape[1]
    group = min(SPREAD_GROUP, tiles)
    smem = pl.BlockSpec(memory_space=pltpu.SMEM)
    total = sum(part.shape[0] for part in parts)
    return pl.pallas_call(
        spread_kernel,
        grid=(tiles // group,),
        in_specs=[smem, smem]
        + [pl.BlockSpec(part.shape, lambda i: (0, 0, 0)) for part in parts]
        + [pl.BlockSpec((group, depth, tile), lambda i: (i, 0, 0))],
        out_specs=pl.BlockSpec((half, group * tile), lambda i: (0, i)),
        out_shape=jax.ShapeDtypeStruct((half, tiles * tile), jnp.bfloat16),
        scratch_shapes=[pltpu.VMEM((total, half, depth), jnp.bfloat16)],
        compiler_params=pltpu.CompilerParams(vmem_limit_bytes=VMEM_LIMIT),
        cost_estimate=cost(2 * half * tiles * tile * depth, 6 * tiles * tile * depth),
        name="spread",
    )(target, place, *parts, blocks)


def in_vmem(kernel, name, out_shape, *args):
    vmem = pl.BlockSpec(memory_space=pltpu.VMEM)
    return pl.pallas_call(
        kernel,
        in_specs=[vmem] * len(args),
        out_specs=vmem,
        out_shape=jax.ShapeDtypeStruct(out_shape, jnp.bfloat16),
        compiler_params=pltpu.CompilerParams(vmem_limit_bytes=VMEM_LIMIT),
        name=name,
    )(*args)


def added(parts):
    total = parts[0].astype(jnp.float32)
    for part in parts[1:]:
        total = total + part.astype(jnp.float32)
    return total


def join_kernel(*refs):
    *parts, out = refs
    first = 0
    for part in parts:
        out[first : first + part.shape[0]] = part[...]
        first += part.shape[0]


def add_kernel(received, out):
    count = out.shape[0]
    for d in range(count):
        parts = [received[first + d] for first in range(0, received.shape[0], count)]
        out[d] = added(parts).astype(jnp.bfloat16)


def split_kernel(received, columns, message):
    sources, own, _ = columns.shape
    outer, peers, rows, _ = message.shape
    total = added([received[z, own:, :] for z in range(sources)]).astype(jnp.bfloat16)
    for z in range(sources):
        columns[z] = received[z, :own, :]
    for x in range(outer):
        for peer in range(peers):
            message[x, peer] = total[x * rows : (x + 1) * rows]


def split(received, own, outer, peers):
    sources, rows, depth = received.shape
    vmem = pl.BlockSpec(memory_space=pltpu.VMEM)
    return pl.pallas_call(
        split_kernel,
        in_specs=[vmem],
        out_specs=[vmem, vmem],
        out_shape=[
            jax.ShapeDtypeStruct((sources, own, depth), jnp.bfloat16),
            jax.ShapeDtypeStruct((outer, peers, (rows - own) // outer, depth), jnp.bfloat16),
        ],
        compiler_params=pltpu.CompilerParams(vmem_limit_bytes=VMEM_LIMIT),
        name="split",
    )(received)


def finish_kernel(scale, received, message):
    for c in range(2):
        total = added([received[s + c] for s in range(0, received.shape[0], 2)]) * scale
        total = total.astype(jnp.bfloat16)
        for peer in range(message.shape[0]):
            message[peer, c] = total


def unpack_kernel(inner, gathered, out):
    n_dom = gathered.shape[0]
    outer = n_dom // inner
    half = out.shape[2] // 2
    each = gathered.shape[2] // CHUNK
    for k in range(out.shape[0]):
        place = k // each
        source = place % outer * inner + place // outer
        rows = slice(k % each * CHUNK, (k % each + 1) * CHUNK)
        first = gathered[source, 0, rows, :].astype(jnp.float32)
        second = gathered[source, 1, rows, :].astype(jnp.float32)
        for g in range(out.shape[1] // CHUNK):
            lanes = slice(g * half, (g + 1) * half)
            out[k, g * CHUNK : (g + 1) * CHUNK, :] = jnp.concatenate(
                [first[:, lanes], second[:, lanes]], 1
            )


def unpack(gathered, offsets, full, inner):
    vmem = pl.BlockSpec(memory_space=pltpu.VMEM)
    return pl.pallas_call(
        functools.partial(unpack_kernel, inner),
        in_specs=[vmem],
        out_specs=vmem,
        out_shape=jax.ShapeDtypeStruct((offsets, full, full), jnp.float32),
        compiler_params=pltpu.CompilerParams(vmem_limit_bytes=VMEM_LIMIT),
        name="unpack",
    )(gathered)


def later(value, lane):
    return jnp.where(lane == 0, 0.0, pltpu.roll(value, 1, 1))


def earlier(value, lane):
    depth = value.shape[1]
    return jnp.where(lane == depth - 1, 0.0, pltpu.roll(value, depth - 1, 1))


def wide_products(weights, values, size, full):
    depth = values.shape[2]
    for x in range(size):
        for y in range(0, size, 2):
            total = None
            for a in range(3):
                window = jnp.concatenate(
                    [values[x + a, (y + i) * full : (y + i + 3) * full, :] for i in range(2)], 1
                )
                product = jnp.dot(weights[a], window, preferred_element_type=jnp.float32)
                total = product if total is None else total + product
            for i in range(2):
                yield x, y + i, total[:, i * depth : (i + 1) * depth]


def conv_kernel_body(chan, grid, wf, wb, latent, message, pp, dd, hh):
    half, depth = grid.shape[2], grid.shape[3]
    full = 2 * half
    n_dom = message.shape[0]

    def cot(c, y, x):
        return grid[c, (12 + y, 27 + 2 * y + x, 27 + 2 * y + x, 48 + y)[x]]

    per = message.shape[1] // CHUNK - 4 * half // CHUNK
    first = pl.multiple_of(chan[0] * half, half)
    for s in range(3):
        for y in range(6):
            for x in range(2):
                for c in range(2):
                    rows = slice(y * full + c * half, y * full + (c + 1) * half)
                    pp[2 * s + x, rows, :] = grid[c, (0, 16, 36)[s] + 2 * y + x]
    lane = lax.broadcasted_iota(jnp.int32, (full, depth), 1)
    for x, y, grown in wide_products(wf, pp, 4, full):
        h = (
            grown[full : 2 * full]
            + later(grown[:full], lane)
            + earlier(grown[2 * full :], lane)
        )
        sig = jax.nn.sigmoid(h)
        upper = jnp.concatenate([cot(0, y, x), cot(1, y, x)], 0).astype(jnp.float32)
        dd[x, y * full : (y + 1) * full, :] = (upper * sig * (1.0 + h * (1.0 - sig))).astype(
            jnp.bfloat16
        )
        if x in (1, 2) and y in (1, 2):
            hh[...] = h * sig
            mine = pp[x + 1, pl.ds((y + 1) * full + first, half), :].astype(jnp.float32)
            latent[:, x - 1, y - 1, :] = (mine + hh[pl.ds(first, half), :]).astype(jnp.bfloat16)
    lane = lax.broadcasted_iota(jnp.int32, (half, depth), 1)
    for x, y, grown in wide_products(wb, dd, 2, full):
        dx = (
            grown[half : 2 * half]
            + earlier(grown[:half], lane)
            + later(grown[2 * half :], lane)
        )
        own = cot(chan[0], y + 1, x + 1).astype(jnp.float32)
        column = (own + dx).astype(jnp.bfloat16)
        for d in range(n_dom):
            message[d, (2 * y + x) * half : (2 * y + x + 1) * half, :] = column
    moved = []
    for x in range(2):
        for y in range(2):
            own = dd[x + 1, pl.ds((y + 1) * full + first, half), :].astype(jnp.float32)
            moved.append(
                jnp.concatenate(
                    [earlier(own, lane), own, later(own, lane), jnp.zeros_like(own)], 0
                ).astype(jnp.bfloat16)
            )
    moved = jnp.concatenate(moved, 1)
    for a in range(3):
        windows = [
            pp[x + 1 + a, (y + 1) * full : (y + 4) * full, :] for x in range(2) for y in range(2)
        ]
        total = lax.dot_general(
            jnp.concatenate(windows, 1),
            moved,
            (((1,), (1,)), ((), ())),
            preferred_element_type=jnp.float32,
        )
        for b in range(3):
            for e in range(3):
                k = 9 * a + 3 * b + e
                pieces = [
                    total[b * full + g * CHUNK : b * full + (g + 1) * CHUNK, e * half : (e + 1) * half]
                    for g in range(full // CHUNK)
                ]
                row = 4 * half + k % per * CHUNK
                message[k // per, row : row + CHUNK, :] = jnp.concatenate(pieces, 1).astype(
                    jnp.bfloat16
                )
    for k in range(27, n_dom * per):
        row = 4 * half + k % per * CHUNK
        message[k // per, row : row + CHUNK, :] = jnp.zeros((CHUNK, depth), jnp.bfloat16)


def conv_layer(chan, grid, wf, wb, n_dom, per):
    half, depth = grid.shape[2], grid.shape[3]
    full = 2 * half
    vmem = pl.BlockSpec(memory_space=pltpu.VMEM)
    return pl.pallas_call(
        conv_kernel_body,
        in_specs=[pl.BlockSpec(memory_space=pltpu.SMEM), vmem, vmem, vmem],
        out_specs=[vmem, vmem],
        out_shape=[
            jax.ShapeDtypeStruct((half, 2, 2, depth), jnp.bfloat16),
            jax.ShapeDtypeStruct((n_dom, 4 * half + per * CHUNK, depth), jnp.bfloat16),
        ],
        scratch_shapes=[
            pltpu.VMEM((6, 6 * full, depth), jnp.bfloat16),
            pltpu.VMEM((4, 4 * full, depth), jnp.bfloat16),
            pltpu.VMEM((full, depth), jnp.float32),
        ],
        compiler_params=pltpu.CompilerParams(vmem_limit_bytes=VMEM_LIMIT),
        name="conv_layer",
    )(chan, grid, wf, wb)


def neighbours(first, last, axis):
    peers = lax.axis_size(axis)
    up = [(i, i + 1) for i in range(peers - 1)]
    down = [(j, i) for i, j in up]
    return lax.ppermute(last, axis, up), lax.ppermute(first, axis, down)


def paired(groups, shift):
    return [(group[i], group[i ^ shift]) for group in groups for i in range(len(group))]


def body(
    point_features,
    neighbour_cells,
    neighbour_weights,
    live_points,
    tile_target,
    conv_kernel,
    cotangent,
):
    half = point_features.shape[0]
    full = 2 * half
    xsize, ysize, depth = cotangent.shape[1:]
    n_dom, n_slab = lax.axis_size("dom"), lax.axis_size("slab")
    width = xsize * ysize
    chan = lax.axis_index("chan").astype(jnp.int32)
    scale = float(width * depth * n_dom * n_slab) ** (-0.5)

    blocks, send = pool(
        tile_target,
        live_points,
        neighbour_cells,
        neighbour_weights,
        point_features,
        n_dom * width,
        depth,
    )

    kernel = conv_kernel.reshape(3, 3, 3, full, full)
    wf = kernel.transpose(0, 2, 4, 1, 3).reshape(3, 3 * full, 3 * full)
    wb = lax.dynamic_slice_in_dim(kernel[::-1, ::-1], chan * half, half, 3)
    wb = wb.transpose(0, 2, 3, 1, 4).reshape(3, 3 * half, 3 * full)

    inner = min(8, n_dom // 2)
    outer = n_dom // inner
    same_z = [[x * inner + z for x in range(outer)] for z in range(inner)]
    same_x = [[x * inner + z for z in range(inner)] for x in range(outer)]

    def exchange(value, axis, groups=None):
        return lax.all_to_all(
            value, axis, split_axis=0, concat_axis=0, tiled=True, axis_index_groups=groups
        )

    def total(value, parts):
        return value.reshape((parts, -1) + value.shape[1:]).astype(jnp.float32).sum(0)

    cot = cotangent.transpose(2, 1, 0, 3)
    part = exchange(send, "dom", same_z)
    part, wf, wb, cot, low, high = lax.optimization_barrier((part, wf, wb, cot, cot[0], cot[-1]))
    part = in_vmem(add_kernel, "add_x", (part.shape[0] // outer,) + part.shape[1:], part)
    part = exchange(part, "dom", same_x)
    pooled = total(part, inner).astype(jnp.bfloat16)

    before, after = neighbours(
        jnp.concatenate([pooled, low], 0), jnp.concatenate([pooled, high], 0), "dom"
    )
    pooled = jnp.concatenate([before[:width], pooled, after[:width]], 0)
    cot = jnp.concatenate([before[None, width:], cot, after[None, width:]], 0)
    before, after = neighbours(
        jnp.concatenate([pooled, cot[:, 0]], 0), jnp.concatenate([pooled, cot[:, -1]], 0), "slab"
    )
    grid = jnp.concatenate([before, pooled, cot.reshape((-1,) + cot.shape[2:]), after], 0)
    grid = lax.all_gather(grid, "chan", axis=0, tiled=False)

    each = -(-27 // n_dom)
    latent, message = conv_layer(chan[None], grid, wf, wb, inner, outer * each)
    message = exchange(message, "dom", same_x)
    peers, rows = 2 * n_slab, each * CHUNK
    columns, kgrad = split(message, width * half, outer, peers)

    same_z_all = [
        [(x * inner + z) * peers + p for x in range(outer) for p in range(peers)]
        for z in range(inner)
    ]
    columns = columns.reshape(inner * width, half, depth)
    parts = [columns, lax.ppermute(columns, "dom", paired(same_z, 1))]
    kgrad = exchange(
        kgrad.reshape(outer * peers, rows, depth), ("dom", "slab", "chan"), same_z_all
    )
    shape = (n_dom, 2, rows, depth)
    kgrad = in_vmem(functools.partial(finish_kernel, scale), "finish", shape, kgrad)
    kgrad = exchange(kgrad, "dom")
    shift = 2
    while shift < outer:
        shape = (shift * parts[0].shape[0],) + parts[0].shape[1:]
        joined = in_vmem(join_kernel, "join", shape, *parts)
        parts.append(lax.ppermute(joined, "dom", paired(same_z, shift)))
        shift = 2 * shift
    place = (lax.axis_index("dom") // inner).astype(jnp.int32)
    feature_grad = spread(tile_target, place[None], parts, blocks)
    kgrad, feature_grad = lax.optimization_barrier((kgrad, feature_grad))
    kernel_grad = unpack(kgrad, 27, full, inner)
    return (latent, feature_grad, kernel_grad)


def solution(mesh):
    placed = (
        P("chan", ("dom", "slab")),
        P(None, ("dom", "slab")),
        P(None, ("dom", "slab")),
        P(("dom", "slab")),
        P(("dom", "slab")),
        P(),
        P("chan", "slab", "dom", None),
    )
    return jax.shard_map(
        body,
        mesh=mesh,
        in_specs=placed,
        out_specs=(P("chan", "slab", "dom", None), P("chan", ("dom", "slab")), P()),
        check_vma=False,
    )
```

```python
import functools

import jax
import jax.numpy as jnp
from jax import lax
from jax.experimental import pallas as pl
from jax.experimental.pallas import tpu as pltpu
from jax.sharding import PartitionSpec as P

POOL_GROUP = 32
SPREAD_GROUP = 32
POOL_VMEM = 60 * 1024 * 1024
VMEM_LIMIT = 16 * 1024 * 1024
CHUNK = 16


def cost(flops, moved):
    return pl.CostEstimate(flops=flops, bytes_accessed=moved, transcendentals=0)


def pool_kernel(target, live, cells, weights, feats, blocks, send, acc):
    step = pl.program_id(0)
    tile = blocks.shape[2]
    depth = blocks.shape[1]

    @pl.when(step == 0)
    def _():
        acc[...] = jnp.zeros_like(acc)

    span = cells.shape[1]
    position = step * span + lax.broadcasted_iota(jnp.int32, cells.shape, 1)
    masked = jnp.where(position < live[0], weights[...], 0.0)
    cell = cells[...].astype(jnp.float32)
    depth_ids = lax.broadcasted_iota(jnp.int32, (depth, tile), 0)
    depth_ids = depth_ids.astype(jnp.float32).astype(jnp.bfloat16)

    def spread_rows(row):
        return jnp.broadcast_to(row, (depth, tile)).astype(jnp.bfloat16)

    for t in range(span // tile):
        cols = slice(t * tile, (t + 1) * tile)
        terms = []
        for k in range(cells.shape[0]):
            weight = spread_rows(masked[k : k + 1, cols])
            here = spread_rows(cell[k : k + 1, cols]) == depth_ids
            terms.append(jnp.where(here, weight, jnp.zeros_like(weight)))
        while len(terms) > 1:
            terms = [one + two for one, two in zip(terms[::2], terms[1::2])]
        block = terms[0]
        blocks[t] = block
        part = lax.dot_general(
            feats[:, cols], block, (((1,), (1,)), ((), ())), preferred_element_type=jnp.float32
        )
        column = target[step * (span // tile) + t]
        acc[column] = acc[column] + part

    @pl.when(step == pl.num_programs(0) - 1)
    def _():
        send[...] = acc[...].astype(jnp.bfloat16)


def pool(target, live, cells, weights, feats, n_columns, depth):
    nbrs, npts = cells.shape
    half = feats.shape[0]
    tiles = target.shape[0]
    tile = npts // tiles
    group = min(POOL_GROUP, tiles)
    span = group * tile
    smem = pl.BlockSpec(memory_space=pltpu.SMEM)
    return pl.pallas_call(
        pool_kernel,
        grid=(tiles // group,),
        in_specs=[
            smem,
            smem,
            pl.BlockSpec((nbrs, span), lambda i: (0, i)),
            pl.BlockSpec((nbrs, span), lambda i: (0, i)),
            pl.BlockSpec((half, span), lambda i: (0, i)),
        ],
        out_specs=[
            pl.BlockSpec((group, depth, tile), lambda i: (i, 0, 0)),
            pl.BlockSpec((n_columns, half, depth), lambda i: (0, 0, 0)),
        ],
        out_shape=[
            jax.ShapeDtypeStruct((tiles, depth, tile), jnp.bfloat16),
            jax.ShapeDtypeStruct((n_columns, half, depth), jnp.bfloat16),
        ],
        scratch_shapes=[pltpu.VMEM((n_columns, half, depth), jnp.float32)],
        compiler_params=pltpu.CompilerParams(vmem_limit_bytes=POOL_VMEM),
        cost_estimate=cost(2 * half * npts * depth, 24 * nbrs * npts * depth // 8),
        name="pool",
    )(target, live, cells, weights, feats)


def spread_kernel(target, place, *refs):
    *parts, blocks, out, columns = refs
    step = pl.program_id(0)
    group, _, tile = blocks.shape
    count = parts[0].shape[0]

    @pl.when(step == 0)
    def _():
        shift = 0
        for part in parts:
            for first in range(0, part.shape[0], count):
                source = jnp.bitwise_xor(place[0], shift)
                columns[pl.ds(source * count, count)] = part[first : first + count]
                shift += 1

    for t in range(group):
        column = target[step * group + t]
        value = jnp.dot(columns[column], blocks[t], preferred_element_type=jnp.float32)
        out[:, t * tile : (t + 1) * tile] = value.astype(jnp.bfloat16)


def spread(target, place, parts, blocks):
    tiles, depth, tile = blocks.shape
    half = parts[0].shape[1]
    group = min(SPREAD_GROUP, tiles)
    smem = pl.BlockSpec(memory_space=pltpu.SMEM)
    total = sum(part.shape[0] for part in parts)
    return pl.pallas_call(
        spread_kernel,
        grid=(tiles // group,),
        in_specs=[smem, smem]
        + [pl.BlockSpec(part.shape, lambda i: (0, 0, 0)) for part in parts]
        + [pl.BlockSpec((group, depth, tile), lambda i: (i, 0, 0))],
        out_specs=pl.BlockSpec((half, group * tile), lambda i: (0, i)),
        out_shape=jax.ShapeDtypeStruct((half, tiles * tile), jnp.bfloat16),
        scratch_shapes=[pltpu.VMEM((total, half, depth), jnp.bfloat16)],
        compiler_params=pltpu.CompilerParams(vmem_limit_bytes=VMEM_LIMIT),
        cost_estimate=cost(2 * half * tiles * tile * depth, 6 * tiles * tile * depth),
        name="spread",
    )(target, place, *parts, blocks)


def in_vmem(kernel, name, out_shape, *args):
    vmem = pl.BlockSpec(memory_space=pltpu.VMEM)
    return pl.pallas_call(
        kernel,
        in_specs=[vmem] * len(args),
        out_specs=vmem,
        out_shape=jax.ShapeDtypeStruct(out_shape, jnp.bfloat16),
        compiler_params=pltpu.CompilerParams(vmem_limit_bytes=VMEM_LIMIT),
        name=name,
    )(*args)


def added(parts):
    total = parts[0].astype(jnp.float32)
    for part in parts[1:]:
        total = total + part.astype(jnp.float32)
    return total


def join_kernel(*refs):
    *parts, out = refs
    first = 0
    for part in parts:
        out[first : first + part.shape[0]] = part[...]
        first += part.shape[0]


def add_kernel(received, out):
    count = out.shape[0]
    for d in range(count):
        parts = [received[first + d] for first in range(0, received.shape[0], count)]
        out[d] = added(parts).astype(jnp.bfloat16)


def split_kernel(received, columns, message):
    sources, own, _ = columns.shape
    outer, peers, rows, _ = message.shape
    total = added([received[z, own:, :] for z in range(sources)]).astype(jnp.bfloat16)
    for z in range(sources):
        columns[z] = received[z, :own, :]
    for x in range(outer):
        for peer in range(peers):
            message[x, peer] = total[x * rows : (x + 1) * rows]


def split(received, own, outer, peers):
    sources, rows, depth = received.shape
    vmem = pl.BlockSpec(memory_space=pltpu.VMEM)
    return pl.pallas_call(
        split_kernel,
        in_specs=[vmem],
        out_specs=[vmem, vmem],
        out_shape=[
            jax.ShapeDtypeStruct((sources, own, depth), jnp.bfloat16),
            jax.ShapeDtypeStruct((outer, peers, (rows - own) // outer, depth), jnp.bfloat16),
        ],
        compiler_params=pltpu.CompilerParams(vmem_limit_bytes=VMEM_LIMIT),
        name="split",
    )(received)


def finish_kernel(scale, received, message):
    for c in range(2):
        total = added([received[s + c] for s in range(0, received.shape[0], 2)]) * scale
        total = total.astype(jnp.bfloat16)
        for peer in range(message.shape[0]):
            message[peer, c] = total


def unpack_kernel(inner, gathered, out):
    n_dom = gathered.shape[0]
    outer = n_dom // inner
    half = out.shape[2] // 2
    each = gathered.shape[2] // CHUNK
    for k in range(out.shape[0]):
        place = k // each
        source = place % outer * inner + place // outer
        rows = slice(k % each * CHUNK, (k % each + 1) * CHUNK)
        first = gathered[source, 0, rows, :].astype(jnp.float32)
        second = gathered[source, 1, rows, :].astype(jnp.float32)
        for g in range(out.shape[1] // CHUNK):
            lanes = slice(g * half, (g + 1) * half)
            out[k, g * CHUNK : (g + 1) * CHUNK, :] = jnp.concatenate(
                [first[:, lanes], second[:, lanes]], 1
            )


def unpack(gathered, offsets, full, inner):
    vmem = pl.BlockSpec(memory_space=pltpu.VMEM)
    return pl.pallas_call(
        functools.partial(unpack_kernel, inner),
        in_specs=[vmem],
        out_specs=vmem,
        out_shape=jax.ShapeDtypeStruct((offsets, full, full), jnp.float32),
        compiler_params=pltpu.CompilerParams(vmem_limit_bytes=VMEM_LIMIT),
        name="unpack",
    )(gathered)


def later(value, lane):
    return jnp.where(lane == 0, 0.0, pltpu.roll(value, 1, 1))


def earlier(value, lane):
    depth = value.shape[1]
    return jnp.where(lane == depth - 1, 0.0, pltpu.roll(value, depth - 1, 1))


def wide_products(weights, values, size, full):
    depth = values.shape[2]
    for x in range(size):
        for y in range(0, size, 2):
            total = None
            for a in range(3):
                window = jnp.concatenate(
                    [values[x + a, (y + i) * full : (y + i + 3) * full, :] for i in range(2)], 1
                )
                product = jnp.dot(weights[a], window, preferred_element_type=jnp.float32)
                total = product if total is None else total + product
            for i in range(2):
                yield x, y + i, total[:, i * depth : (i + 1) * depth]


def conv_kernel_body(chan, grid, wf, wb, latent, message, pp, dd, hh):
    half, depth = grid.shape[2], grid.shape[3]
    full = 2 * half
    n_dom = message.shape[0]

    def cot(c, y, x):
        return grid[c, (12 + y, 27 + 2 * y + x, 27 + 2 * y + x, 48 + y)[x]]

    per = message.shape[1] // CHUNK - 4 * half // CHUNK
    first = pl.multiple_of(chan[0] * half, half)
    for s in range(3):
        for y in range(6):
            for x in range(2):
                for c in range(2):
                    rows = slice(y * full + c * half, y * full + (c + 1) * half)
                    pp[2 * s + x, rows, :] = grid[c, (0, 16, 36)[s] + 2 * y + x]
    lane = lax.broadcasted_iota(jnp.int32, (full, depth), 1)
    for x, y, grown in wide_products(wf, pp, 4, full):
        h = (
            grown[full : 2 * full]
            + later(grown[:full], lane)
            + earlier(grown[2 * full :], lane)
        )
        sig = jax.nn.sigmoid(h)
        upper = jnp.concatenate([cot(0, y, x), cot(1, y, x)], 0).astype(jnp.float32)
        dd[x, y * full : (y + 1) * full, :] = (upper * sig * (1.0 + h * (1.0 - sig))).astype(
            jnp.bfloat16
        )
        if x in (1, 2) and y in (1, 2):
            hh[...] = h * sig
            mine = pp[x + 1, pl.ds((y + 1) * full + first, half), :].astype(jnp.float32)
            latent[:, x - 1, y - 1, :] = (mine + hh[pl.ds(first, half), :]).astype(jnp.bfloat16)
    lane = lax.broadcasted_iota(jnp.int32, (half, depth), 1)
    for x, y, grown in wide_products(wb, dd, 2, full):
        dx = (
            grown[half : 2 * half]
            + earlier(grown[:half], lane)
            + later(grown[2 * half :], lane)
        )
        own = cot(chan[0], y + 1, x + 1).astype(jnp.float32)
        column = (own + dx).astype(jnp.bfloat16)
        for d in range(n_dom):
            message[d, (2 * y + x) * half : (2 * y + x + 1) * half, :] = column
    moved = []
    for x in range(2):
        for y in range(2):
            own = dd[x + 1, pl.ds((y + 1) * full + first, half), :].astype(jnp.float32)
            moved.append(
                jnp.concatenate(
                    [earlier(own, lane), own, later(own, lane), jnp.zeros_like(own)], 0
                ).astype(jnp.bfloat16)
            )
    moved = jnp.concatenate(moved, 1)
    for a in range(3):
        windows = [
            pp[x + 1 + a, (y + 1) * full : (y + 4) * full, :] for x in range(2) for y in range(2)
        ]
        total = lax.dot_general(
            jnp.concatenate(windows, 1),
            moved,
            (((1,), (1,)), ((), ())),
            preferred_element_type=jnp.float32,
        )
        for b in range(3):
            for e in range(3):
                k = 9 * a + 3 * b + e
                pieces = [
                    total[b * full + g * CHUNK : b * full + (g + 1) * CHUNK, e * half : (e + 1) * half]
                    for g in range(full // CHUNK)
                ]
                row = 4 * half + k % per * CHUNK
                message[k // per, row : row + CHUNK, :] = jnp.concatenate(pieces, 1).astype(
                    jnp.bfloat16
                )
    for k in range(27, n_dom * per):
        row = 4 * half + k % per * CHUNK
        message[k // per, row : row + CHUNK, :] = jnp.zeros((CHUNK, depth), jnp.bfloat16)


def conv_layer(chan, grid, wf, wb, n_dom, per):
    half, depth = grid.shape[2], grid.shape[3]
    full = 2 * half
    vmem = pl.BlockSpec(memory_space=pltpu.VMEM)
    return pl.pallas_call(
        conv_kernel_body,
        in_specs=[pl.BlockSpec(memory_space=pltpu.SMEM), vmem, vmem, vmem],
        out_specs=[vmem, vmem],
        out_shape=[
            jax.ShapeDtypeStruct((half, 2, 2, depth), jnp.bfloat16),
            jax.ShapeDtypeStruct((n_dom, 4 * half + per * CHUNK, depth), jnp.bfloat16),
        ],
        scratch_shapes=[
            pltpu.VMEM((6, 6 * full, depth), jnp.bfloat16),
            pltpu.VMEM((4, 4 * full, depth), jnp.bfloat16),
            pltpu.VMEM((full, depth), jnp.float32),
        ],
        compiler_params=pltpu.CompilerParams(vmem_limit_bytes=VMEM_LIMIT),
        name="conv_layer",
    )(chan, grid, wf, wb)


def neighbours(first, last, axis):
    peers = lax.axis_size(axis)
    up = [(i, i + 1) for i in range(peers - 1)]
    down = [(j, i) for i, j in up]
    return lax.ppermute(last, axis, up), lax.ppermute(first, axis, down)


def paired(groups, shift):
    return [(group[i], group[i ^ shift]) for group in groups for i in range(len(group))]


def body(
    point_features,
    neighbour_cells,
    neighbour_weights,
    live_points,
    tile_target,
    conv_kernel,
    cotangent,
):
    half = point_features.shape[0]
    full = 2 * half
    xsize, ysize, depth = cotangent.shape[1:]
    n_dom, n_slab = lax.axis_size("dom"), lax.axis_size("slab")
    width = xsize * ysize
    chan = lax.axis_index("chan").astype(jnp.int32)
    scale = float(width * depth * n_dom * n_slab) ** (-0.5)

    blocks, send = pool(
        tile_target,
        live_points,
        neighbour_cells,
        neighbour_weights,
        point_features,
        n_dom * width,
        depth,
    )

    kernel = conv_kernel.reshape(3, 3, 3, full, full)
    wf = kernel.transpose(0, 2, 4, 1, 3).reshape(3, 3 * full, 3 * full)
    wb = lax.dynamic_slice_in_dim(kernel[::-1, ::-1], chan * half, half, 3)
    wb = wb.transpose(0, 2, 3, 1, 4).reshape(3, 3 * half, 3 * full)

    inner = min(8, n_dom // 2)
    outer = n_dom // inner
    same_z = [[x * inner + z for x in range(outer)] for z in range(inner)]
    same_x = [[x * inner + z for z in range(inner)] for x in range(outer)]

    def exchange(value, axis, groups=None):
        return lax.all_to_all(
            value, axis, split_axis=0, concat_axis=0, tiled=True, axis_index_groups=groups
        )

    def total(value, parts):
        return value.reshape((parts, -1) + value.shape[1:]).astype(jnp.float32).sum(0)

    cot = cotangent.transpose(2, 1, 0, 3)
    part = exchange(send, "dom", same_z)
    part, wf, wb, cot, low, high = lax.optimization_barrier((part, wf, wb, cot, cot[0], cot[-1]))
    part = in_vmem(add_kernel, "add_x", (part.shape[0] // outer,) + part.shape[1:], part)
    part = exchange(part, "dom", same_x)
    pooled = total(part, inner).astype(jnp.bfloat16)

    before, after = neighbours(
        jnp.concatenate([pooled, low], 0), jnp.concatenate([pooled, high], 0), "dom"
    )
    pooled = jnp.concatenate([before[:width], pooled, after[:width]], 0)
    cot = jnp.concatenate([before[None, width:], cot, after[None, width:]], 0)
    before, after = neighbours(
        jnp.concatenate([pooled, cot[:, 0]], 0), jnp.concatenate([pooled, cot[:, -1]], 0), "slab"
    )
    grid = jnp.concatenate([before, pooled, cot.reshape((-1,) + cot.shape[2:]), after], 0)
    grid = lax.all_gather(grid, "chan", axis=0, tiled=False)

    each = -(-27 // n_dom)
    latent, message = conv_layer(chan[None], grid, wf, wb, inner, outer * each)
    message = exchange(message, "dom", same_x)
    peers, rows = 2 * n_slab, each * CHUNK
    columns, kgrad = split(message, width * half, outer, peers)

    same_z_all = [
        [(x * inner + z) * peers + p for x in range(outer) for p in range(peers)]
        for z in range(inner)
    ]
    columns = columns.reshape(inner * width, half, depth)
    parts = [columns, lax.ppermute(columns, "dom", paired(same_z, 1))]
    kgrad = exchange(
        kgrad.reshape(outer * peers, rows, depth), ("dom", "slab", "chan"), same_z_all
    )
    shape = (n_dom, 2, rows, depth)
    kgrad = in_vmem(functools.partial(finish_kernel, scale), "finish", shape, kgrad)
    kgrad = exchange(kgrad, "dom")
    shift = 2
    while shift < outer:
        shape = (shift * parts[0].shape[0],) + parts[0].shape[1:]
        joined = in_vmem(join_kernel, "join", shape, *parts)
        parts.append(lax.ppermute(joined, "dom", paired(same_z, shift)))
        shift = 2 * shift
    place = (lax.axis_index("dom") // inner).astype(jnp.int32)
    feature_grad = spread(tile_target, place[None], parts, blocks)
    kgrad, feature_grad = lax.optimization_barrier((kgrad, feature_grad))
    kernel_grad = unpack(kgrad, 27, full, inner)
    return (latent, feature_grad, kernel_grad)


def solution(mesh):
    placed = (
        P("chan", ("dom", "slab")),
        P(None, ("dom", "slab")),
        P(None, ("dom", "slab")),
        P(("dom", "slab")),
        P(("dom", "slab")),
        P(),
        P("chan", "slab", "dom", None),
    )
    return jax.shard_map(
        body,
        mesh=mesh,
        in_specs=placed,
        out_specs=(P("chan", "slab", "dom", None), P("chan", ("dom", "slab")), P()),
        check_vma=False,
    )
```
